32 devices in a mesh: gx: 8 (over z, core), gy: 4 (over y, x).
Axes of the slice: x: 2, y: 2, z: 4, core: 2. Of those that a mesh axis runs over, the one named last changes fastest.
Arguments:
- adjoint_field: float32 [3, 8, 4, 64, 512], P(None, 'gx', 'gy'), may hold values from -12 to 27
- velocity: bfloat16 [3, 8, 4, 64, 512], P(None, 'gx', 'gy'), may hold values from -1.1953125 to 1.1953125
- diffusivity: float32 [3, 8, 4, 64, 512], P(None, 'gx', 'gy'), may hold values from 0.3 to 3
- jacobian: float32 [8, 4, 64, 512], P('gx', 'gy'), may hold values from 0.5 to 2
- element_slot: int32 [8, 4, 64], P('gx', 'gy'), may hold values from 0 to 63, each once within a row
Outputs:
- adjoint_prev: float32 [3, 8, 4, 64, 512], P(None, 'gx', 'gy')
The draws below stay inside these ranges and needn't reach their ends.
Inputs may be any that keep to these rules, and one draw needn't show every extreme that they name: Each partition's row of element_slot is a permutation of 0 to 63.
All inputs are finite; a program needn't handle non-finite values.
Results may differ from the reference program's by a relative error of at most 0.0003.
Values sent between devices are 32-bit elements; how exact they have to be, the bound alone decides.
A program may use at most 64 MiB of HBM per device.

```python
import math
import jax
import jax.numpy as jnp
import numpy as np
from jax import lax

EX = 2
EY = 2
EZ = 16
ITERS = 4
E_DEV = 64
PARTS_X = 8
PARTS_Y = 4


def draw_adjoint_field(key, part):
    shape = (3, PARTS_X, PARTS_Y, E_DEV, 512)
    rough = jax.random.truncated_normal(key, -4.0, 4.0, shape, jnp.float32)
    along_x = jnp.exp(jnp.linspace(0.0, math.log(3.0), PARTS_X))
    scaling = jnp.broadcast_to(along_x[None, :, None, None, None], shape)
    return rough * scaling


def block_levels(key, extent, shards, least, top_value):
    gain = 1.0
    for axis_at, shards_of in shards:
        steps = jax.random.uniform(jax.random.fold_in(jax.random.fold_in(key, 6), axis_at), (shards_of,), jnp.float32, least / len(shards), top_value / len(shards))
        gain = gain * jnp.repeat(jnp.exp(steps), extent[axis_at] // shards_of).reshape((-1,) + (1,) * (len(extent) - 1 - axis_at))
    return gain


def scatter_about(rng, shape, scale, most, split=(), held_as=jnp.bfloat16):
    entries = scale * jax.random.normal(rng, shape, jnp.float32)
    if split:
        entries = entries * block_levels(rng, shape, split, -0.22, 0.18)
    return jnp.clip(entries, -most, most).astype(held_as)


def setup_inputs(seed: int = 0) -> dict:
    streams_of = jax.random.split(jax.random.key(seed), 6)
    adjoint_field = draw_adjoint_field(jax.random.fold_in(streams_of[5], 71), 0)
    velocity = scatter_about(streams_of[1], (3, PARTS_X, PARTS_Y, E_DEV, 512), 0.2, 1.1953125, ((1, 8), (2, 4)))
    diffusivity = jnp.clip(jnp.exp(math.log(3.0) - 2.3025851 * jax.random.uniform(streams_of[2], (3, PARTS_X, PARTS_Y, E_DEV, 512), jnp.float32) ** block_levels(streams_of[2], (3, PARTS_X, PARTS_Y, E_DEV, 512), ((1, 8), (2, 4)), -0.2, 0.2)), 0.3, 3.0)
    jacobian = jnp.clip(jnp.exp(math.log(2.0) - 1.3862944 * jax.random.uniform(streams_of[3], (PARTS_X, PARTS_Y, E_DEV, 512), jnp.float32) ** block_levels(streams_of[3], (PARTS_X, PARTS_Y, E_DEV, 512), ((0, 8), (1, 4)), -0.2, 0.2)), 0.5, 2.0)
    element_slot = jax.vmap(lambda own: jax.random.permutation(own, E_DEV))(jax.random.split(streams_of[4], PARTS_X * PARTS_Y)).reshape((PARTS_X, PARTS_Y, E_DEV)).astype(jnp.int32)
    return dict(adjoint_field=adjoint_field, velocity=velocity, diffusivity=diffusivity, jacobian=jacobian, element_slot=element_slot)


time_step = 0.25


def legendre_seven(points):
    previous = points * 0.0 + 1.0
    current = points
    for degree in range(1, 7):
        following = ((2 * degree + 1) * points * current - degree * previous) / (degree + 1)
        previous = current
        current = following
    return current


def gll_tables():
    poly_order = 7
    points = np.array([-1.0, -0.8717401485096066, -0.5917001814331423, -0.2092992179024789,
                       0.2092992179024789, 0.5917001814331423, 0.8717401485096066, 1.0])
    end_values = legendre_seven(points)
    weights = 2.0 / (poly_order * (poly_order + 1) * end_values ** 2)
    spread = points[:, None] - points[None, :]
    identity = np.eye(poly_order + 1)
    diff_table = end_values[:, None] / (end_values[None, :] * (spread + identity))
    diff_table = diff_table * (1.0 - identity)
    corners = np.zeros(poly_order + 1)
    corners[0] = -poly_order * (poly_order + 1) / 4.0
    corners[-1] = poly_order * (poly_order + 1) / 4.0
    diff_table = diff_table + identity * corners[None, :]
    return weights.astype(np.float32), diff_table.astype(np.float32)


def weight_outer(weights):
    return weights[:, None, None] * weights[None, :, None] * weights[None, None, :]


def fold_pair(values_in, position):
    moved = jnp.moveaxis(values_in, (position, position + 1), (-2, -1))
    leading = moved.shape[:-2]
    number = moved.shape[-2]
    body_part = moved[..., :7].reshape(leading + (7 * number,))
    body_part = jnp.concatenate([body_part, jnp.zeros(leading + (1,), moved.dtype)], axis=-1)
    padding = [(0, 0)] * len(leading) + [(1, 0), (0, 6)]
    trailing = jnp.pad(moved[..., 7:8], padding).reshape(leading + (7 * number + 7,))[..., : 7 * number + 1]
    return jnp.moveaxis(body_part + trailing, -1, position)


def unfold_pair(values_in, position):
    moved = jnp.moveaxis(values_in, position, -1)
    leading = moved.shape[:-1]
    number = (moved.shape[-1] - 1) // 7
    body_part = moved[..., : 7 * number].reshape(leading + (number, 7))
    trailing = moved[..., 7::7][..., None]
    joined = jnp.concatenate([body_part, trailing], axis=-1)
    return jnp.moveaxis(joined, (-2, -1), (position, position + 1))


def assemble(element_vals):
    sectioned = jnp.transpose(element_vals, (0, 1, 4, 2, 5, 3, 6))
    sectioned = fold_pair(sectioned, 5)
    sectioned = fold_pair(sectioned, 3)
    return fold_pair(sectioned, 1)


def spread_out(unique_grid):
    sectioned = unfold_pair(unique_grid, 1)
    sectioned = unfold_pair(sectioned, 3)
    sectioned = unfold_pair(sectioned, 5)
    return jnp.transpose(sectioned, (0, 1, 3, 5, 2, 4, 6))


def grid_form(values_in, slot_list):
    comps = values_in.shape[0]
    inverse = jnp.argsort(slot_list, axis=-1).astype(jnp.int32)
    picker = jnp.broadcast_to(inverse[None, :, :, :, None], values_in.shape)
    ordered = jnp.take_along_axis(values_in, picker, axis=3)
    shaped = ordered.reshape(comps, PARTS_X, PARTS_Y, EX, EY, EZ, 8, 8, 8)
    shaped = jnp.transpose(shaped, (0, 1, 3, 2, 4, 5, 6, 7, 8))
    return shaped.reshape(comps, PARTS_X * EX, PARTS_Y * EY, EZ, 8, 8, 8)


def stored_form(values_in, slot_list):
    comps = values_in.shape[0]
    shaped = values_in.reshape(comps, PARTS_X, EX, PARTS_Y, EY, EZ, 512)
    shaped = jnp.transpose(shaped, (0, 1, 3, 2, 4, 5, 6)).reshape(comps, PARTS_X, PARTS_Y, E_DEV, 512)
    picker = jnp.broadcast_to(slot_list[None, :, :, :, None].astype(jnp.int32), shaped.shape)
    return jnp.take_along_axis(shaped, picker, axis=3)


def derive(values_in, diff_table, direction, flip):
    matrix = diff_table.T if flip else diff_table
    forms = ("ai,...ijk->...ajk", "aj,...ijk->...iak", "ak,...ijk->...ija")
    return jnp.einsum(forms[direction], matrix, values_in, precision=lax.Precision.HIGHEST)


def reference(adjoint_field, velocity, diffusivity, jacobian, element_slot):
    weights, table_np = gll_tables()
    diff_table = jnp.asarray(table_np)
    weight_cube = jnp.asarray(weight_outer(weights))
    adjoint = grid_form(adjoint_field, element_slot)
    flow = grid_form(velocity.astype(jnp.float32), element_slot)
    conduct = grid_form(diffusivity, element_slot)
    mass_term = grid_form(jacobian[None], element_slot)[0] * weight_cube

    def deriv(values_in, direction):
        return derive(values_in, diff_table, direction, False)

    rotation = jnp.stack([
        deriv(adjoint[2], 1) - deriv(adjoint[1], 2),
        deriv(adjoint[0], 2) - deriv(adjoint[2], 0),
        deriv(adjoint[1], 0) - deriv(adjoint[0], 1)])
    induced = jnp.stack([
        flow[1] * rotation[2] - flow[2] * rotation[1],
        flow[2] * rotation[0] - flow[0] * rotation[2],
        flow[0] * rotation[1] - flow[1] * rotation[0]])
    source = mass_term * (adjoint + time_step * induced)
    right_side = assemble(source)

    def operate(vector):
        element_vals = spread_out(vector)
        stiffness = jnp.zeros_like(element_vals)
        for direction in range(3):
            fluxes = weight_cube * conduct[direction] * derive(element_vals, diff_table, direction, False)
            stiffness = stiffness + derive(fluxes, diff_table, direction, True)
        return assemble(mass_term * element_vals + time_step * stiffness)

    solution = jnp.zeros_like(right_side)
    residual = right_side
    direction_vec = right_side
    norm_now = jnp.sum(residual * residual)
    for step_index in range(ITERS):
        applied = operate(direction_vec)
        step_len = norm_now / jnp.sum(direction_vec * applied)
        solution = solution + step_len * direction_vec
        residual = residual - step_len * applied
        norm_next = jnp.sum(residual * residual)
        direction_vec = residual + (norm_next / norm_now) * direction_vec
        norm_now = norm_next
    return stored_form(spread_out(solution), element_slot)
```

```python
import functools

import jax
import jax.numpy as jnp
import numpy as np
from jax import lax
from jax.experimental import pallas as pl
from jax.experimental.pallas import tpu as pltpu
from jax.sharding import PartitionSpec as P

EX = 2
EY = 2
EZ = 16
ITERS = 4

time_step = 0.25
MESH = pl.DeviceIdType.MESH
f32 = jnp.float32
bf16 = jnp.bfloat16

SIDES = ((-1, 0), (1, 0), (0, -1), (0, 1))
CORNERS = ((-1, -1), (-1, 1), (1, -1), (1, 1))


def legendre_seven(points):
    previous = points * 0.0 + 1.0
    current = points
    for degree in range(1, 7):
        following = ((2 * degree + 1) * points * current - degree * previous) / (degree + 1)
        previous = current
        current = following
    return current


def gll_tables():
    poly_order = 7
    points = np.array(
        [
            -1.0,
            -0.8717401485096066,
            -0.5917001814331423,
            -0.2092992179024789,
            0.2092992179024789,
            0.5917001814331423,
            0.8717401485096066,
            1.0,
        ]
    )
    end_values = legendre_seven(points)
    weights = 2.0 / (poly_order * (poly_order + 1) * end_values**2)
    spread = points[:, None] - points[None, :]
    identity = np.eye(poly_order + 1)
    diff_table = end_values[:, None] / (end_values[None, :] * (spread + identity))
    diff_table = diff_table * (1.0 - identity)
    corners = np.zeros(poly_order + 1)
    corners[0] = -poly_order * (poly_order + 1) / 4.0
    corners[-1] = poly_order * (poly_order + 1) / 4.0
    diff_table = diff_table + identity * corners[None, :]
    return (weights.astype(np.float32), diff_table.astype(np.float32))


def halves(table):
    high = table.astype(jnp.bfloat16)
    low = (table - high.astype(np.float32)).astype(jnp.bfloat16)
    return high, low


def constant_tables():
    weights, diff = gll_tables()
    eye = np.eye(8, dtype=np.float32)
    pair = np.eye(2, dtype=np.float32)
    along_j = np.kron(pair, np.kron(diff.T, eye))
    along_k = np.kron(pair, np.kron(eye, diff.T))
    forward = np.concatenate([along_j, along_k], axis=1)
    f_high, f_low = halves(forward)
    b_high, b_low = halves(np.ascontiguousarray(forward.T))
    forward_high = np.concatenate([f_high, f_high], axis=0)
    backward_both = np.concatenate([b_high, b_low], axis=1)
    coef = np.zeros((2, 2, 4, 4, 128), np.float32)
    for flip in range(2):
        matrix = diff.T if flip else diff
        for out in range(4):
            for inn in range(4):
                for il in range(2):
                    span = slice(il * 64, il * 64 + 64)
                    coef[flip, 0, out, inn, span] = matrix[2 * out + il, 2 * inn + il]
                    coef[flip, 1, out, inn, span] = matrix[2 * out + il, 2 * inn + 1 - il]
    coef = coef.reshape(64, 128)
    cube = weights[:, None, None] * weights[None, :, None] * weights[None, None, :]
    return forward_high, f_low, backward_both, b_high, coef, cube.reshape(4, 128).astype(np.float32)


def dot(a, b):
    return jnp.dot(a, b, preferred_element_type=f32)


def split(values):
    high = values.astype(bf16)
    return high, (values - high.astype(f32)).astype(bf16)


def roll(values, shift, axis=None):
    axis = values.ndim - 1 if axis is None else axis
    shift = shift % values.shape[axis]
    return values if shift == 0 else pltpu.roll(values, shift, axis)


def kernel(
    nx,
    ny,
    adj_ref,
    vel_ref,
    dif_ref,
    jac_ref,
    slot_ref,
    fh_ref,
    fl_ref,
    bb_ref,
    bh_ref,
    coef_ref,
    cube_ref,
    out_ref,
    mass,
    cond,
    share,
    w,
    res,
    dire,
    along,
    sol,
    face_out,
    face_in,
    corner_out,
    corner_in,
    sums,
    face_s,
    face_r,
    corner_s,
    corner_r,
    sums_s,
    sums_r,
):
    gx = lax.axis_index("gx")
    gy = lax.axis_index("gy")
    total = nx * ny
    me = gx * ny + gy
    cells = EX * EY * EZ

    face_in[...] = jnp.zeros_like(face_in)
    corner_in[...] = jnp.zeros_like(corner_in)

    barrier = pltpu.get_barrier_semaphore()

    def greet(step, carry):
        other = lax.rem(me + step, total)
        pl.semaphore_signal(
            barrier, inc=1, device_id=(other // ny, lax.rem(other, ny)), device_id_type=MESH
        )
        return carry

    lax.fori_loop(1, total, greet, 0)

    lane = lax.broadcasted_iota(jnp.int32, (1, 128), 1)
    lane_k = lane % 8
    lane_j = (lane // 8) % 8
    lane_i = lane // 64
    group = lane // 8

    place = lax.broadcasted_iota(jnp.int32, (cells, cells), 0)
    picks = (jnp.broadcast_to(slot_ref[...], (cells, cells)) == place).astype(f32)
    pick = picks.astype(bf16)

    def to_brick(stored):
        high, rest = split(stored)
        low = rest
        third = (stored - high.astype(f32) - low.astype(f32)).astype(bf16)
        return dot(pick, high) + dot(pick, low) + dot(pick, third)

    def rows(values):
        return values.reshape(values.shape[0] * values.shape[1], 128)

    def derive_jk(values):
        high, low = split(values)
        both = dot(jnp.concatenate([high, low], axis=1), fh_ref[...]) + dot(high, fl_ref[...])
        return both[:, :128], both[:, 128:]

    def derive_i(parts, flip):
        turned = [roll(part, 64) for part in parts]
        outs = []
        for out in range(4):
            acc = None
            for inn in range(4):
                at = flip * 32 + out * 4 + inn
                term = parts[inn] * coef_ref[at : at + 1, :]
                term = term + turned[inn] * coef_ref[at + 16 : at + 17, :]
                acc = term if acc is None else acc + term
            outs.append(acc)
        return outs

    adj = [to_brick(adj_ref[c]) for c in range(3)]
    for h in range(4):
        for c in range(3):
            w[h, c] = adj[c][:, h * 128 : h * 128 + 128].reshape(EX, EY, EZ, 128)
    jac = to_brick(jac_ref[0])
    for h in range(4):
        weight = cube_ref[h : h + 1, :]
        mass[h] = jac[:, h * 128 : h * 128 + 128] * weight
    for m in range(3):
        con = to_brick(dif_ref[m])
        for h in range(4):
            weight = time_step * cube_ref[h : h + 1, :]
            cond[m, h] = con[:, h * 128 : h * 128 + 128] * weight

    first_x = jnp.where(gx > 0, 0.5, 1.0).astype(f32)
    last_x = jnp.where(gx < nx - 1, 0.5, 1.0).astype(f32)
    first_y = jnp.where(gy > 0, 0.5, 1.0).astype(f32)
    last_y = jnp.where(gy < ny - 1, 0.5, 1.0).astype(f32)
    row_z = lax.broadcasted_iota(jnp.int32, (EZ, 128), 0)
    lane_z = lax.broadcasted_iota(jnp.int32, (EZ, 128), 1)
    k_z = lane_z % 8
    half_z = ((k_z == 0) & (row_z > 0)) | ((k_z == 7) & (row_z < EZ - 1))
    share_z = jnp.where(half_z, 0.5, 1.0).astype(f32)
    for x in range(EX):
        low_x = first_x if x == 0 else 0.5
        top_x = last_x if x == EX - 1 else 0.5
        for y in range(EY):
            low_y = first_y if y == 0 else 0.5
            top_y = last_y if y == EY - 1 else 0.5
            share_y = jnp.where(lane_j == 0, low_y, jnp.where(lane_j == 7, top_y, 1.0))
            for h in range(4):
                share_x = jnp.ones((1, 128), f32)
                if h == 0:
                    share_x = jnp.where(lane_i == 0, low_x, 1.0)
                if h == 3:
                    share_x = jnp.where(lane_i == 1, top_x, 1.0)
                at = (x * EY + y) * EZ
                share[h, at : at + EZ] = share_z * (share_x * share_y)

    dire[...] = jnp.zeros_like(dire)
    along[...] = jnp.zeros_like(along)
    sol[...] = jnp.zeros_like(sol)

    full = w[...].reshape(4, 3, cells, 128)
    grad_j, grad_k = derive_jk(full.reshape(12 * cells, 128))
    grad_j = grad_j.reshape(4, 3, cells, 128)
    grad_k = grad_k.reshape(4, 3, cells, 128)
    grad_i = [derive_i([full[h, c] for h in range(4)], 0) for c in range(3)]
    flow = [dot(pick, vel_ref[c]) for c in range(3)]
    for h in range(4):
        at = slice(h * 128, h * 128 + 128)
        v = [flow[c][:, at] for c in range(3)]
        r = [
            grad_j[h, 2] - grad_k[h, 1],
            grad_k[h, 0] - grad_i[2][h],
            grad_i[1][h] - grad_j[h, 0],
        ]
        for c in range(3):
            c1, c2 = (c + 1) % 3, (c + 2) % 3
            value = full[h, c] + time_step * (v[c1] * r[c2] - v[c2] * r[c1])
            w[h, c] = (mass[h] * value).reshape(EX, EY, EZ, 128)

    pl.semaphore_wait(barrier, total - 1)

    def exists(side):
        ax, ay = gx + side[0], gy + side[1]
        return (ax >= 0) & (ax < nx) & (ay >= 0) & (ay < ny)

    def copies(turn):
        made = []
        for d, side in enumerate(SIDES):
            made.append(
                (
                    side,
                    pltpu.make_async_remote_copy(
                        src_ref=face_out.at[turn, d],
                        dst_ref=face_in.at[turn, d],
                        send_sem=face_s.at[turn, d],
                        recv_sem=face_r.at[turn, d],
                        device_id=(gx + side[0], gy + side[1]),
                        device_id_type=MESH,
                    ),
                )
            )
        for d, side in enumerate(CORNERS):
            made.append(
                (
                    side,
                    pltpu.make_async_remote_copy(
                        src_ref=corner_out.at[turn, d],
                        dst_ref=corner_in.at[turn, d],
                        send_sem=corner_s.at[turn, d],
                        recv_sem=corner_r.at[turn, d],
                        device_id=(gx + side[0], gy + side[1]),
                        device_id_type=MESH,
                    ),
                )
            )
        return made

    def corner_spot(side):
        h = 0 if side[0] < 0 else 3
        x = 0 if side[0] < 0 else EX - 1
        y = 0 if side[1] < 0 else EY - 1
        base = (0 if side[0] < 0 else 64) + (0 if side[1] < 0 else 56)
        return h, x, y, base

    def fold_inside():
        values = w[...].reshape(12 * cells, 128)
        count = 12 * cells
        zed = lax.broadcasted_iota(jnp.int32, (EZ, 128), 0)
        kay = lax.broadcasted_iota(jnp.int32, (EZ, 128), 1) % 8
        upper = ((kay == 7) & (zed < EZ - 1)).astype(f32)
        lower = ((kay == 0) & (zed > 0)).astype(f32)
        from_next = roll(roll(values, 7), count - 1, 0).reshape(12 * EX * EY, EZ, 128)
        from_last = roll(roll(values, -7), 1, 0).reshape(12 * EX * EY, EZ, 128)
        values = values.reshape(12 * EX * EY, EZ, 128)
        values = values + from_next * upper[None] + from_last * lower[None]
        values = values.reshape(4, 3, EX, EY, EZ, 128)
        is_top = lane_j == 7
        is_low = lane_j == 0
        columns = [values[:, :, :, y] for y in range(EY)]
        folded = list(columns)
        for y in range(EY - 1):
            folded[y] = folded[y] + jnp.where(is_top, roll(columns[y + 1], 56), 0.0)
            folded[y + 1] = folded[y + 1] + jnp.where(is_low, roll(columns[y], -56), 0.0)
        for y in range(EY):
            w[:, :, :, y] = folded[y]
        for x in range(EX - 1):
            left = w[3, :, x]
            right = w[0, :, x + 1]
            w[3, :, x] = left + jnp.where(lane_i == 1, roll(right, 64), 0.0)
            w[0, :, x + 1] = right + jnp.where(lane_i == 0, roll(left, 64), 0.0)

    def send_faces(turn):
        left = w[0, :, 0]
        face_out[turn, 0] = jnp.where(lane_i == 0, left[:, 0], roll(left[:, 1], 64))
        right = w[3, :, EX - 1]
        face_out[turn, 1] = jnp.where(lane_i == 0, roll(right[:, 0], 64), right[:, 1])
        for d, y, j in ((2, 0, 0), (3, EY - 1, 7)):
            acc = None
            for h in range(4):
                for x in range(EX):
                    part = jnp.where(lane_j == j, w[h, :, x, y], 0.0)
                    part = roll(part, h * 8 + x * 32 - j * 8)
                    acc = part if acc is None else acc + part
            face_out[turn, d] = acc
        for d, side in enumerate(CORNERS):
            h, x, y, base = corner_spot(side)
            acc = None
            for c in range(3):
                part = jnp.where(group == base // 8, w[h, c, x, y], 0.0)
                part = roll(part, c * 8 - base)
                acc = part if acc is None else acc + part
            corner_out[turn, d] = acc
        for side, copy in copies(turn):
            pl.when(exists(side))(copy.start)

    def take_faces(turn):
        for side, copy in copies(turn):
            pl.when(exists((-side[0], -side[1])))(copy.wait_recv)
        left = face_in[turn, 1]
        right = face_in[turn, 0]
        for h, x, arrived, here in ((0, 0, left, 0), (3, EX - 1, right, 1)):
            turned = roll(arrived, 64)
            pair = (arrived, turned) if here == 0 else (turned, arrived)
            for y in range(EY):
                w[h, :, x, y] = w[h, :, x, y] + jnp.where(lane_i == here, pair[y], 0.0)
        for d, y, j in ((3, 0, 0), (2, EY - 1, 7)):
            arrived = face_in[turn, d]
            for h in range(4):
                for x in range(EX):
                    part = roll(arrived, j * 8 - h * 8 - x * 32)
                    w[h, :, x, y] = w[h, :, x, y] + jnp.where(lane_j == j, part, 0.0)
        for d, side in enumerate(CORNERS):
            h, x, y, base = corner_spot((-side[0], -side[1]))
            arrived = corner_in[turn, d]
            for c in range(3):
                part = roll(arrived, base - c * 8)
                w[h, c, x, y] = w[h, c, x, y] + jnp.where(group == base // 8, part, 0.0)

    def sent_faces(turn):
        for side, copy in copies(turn):
            pl.when(exists(side))(copy.wait_send)

    fold_inside()
    send_faces(0)
    take_faces(0)
    sent_faces(0)
    res[...] = w[...]

    def sum_copy(turn, step):
        other = lax.rem(me + step, total)
        return pltpu.make_async_remote_copy(
            src_ref=sums.at[turn, me],
            dst_ref=sums.at[turn, me],
            send_sem=sums_s.at[turn],
            recv_sem=sums_r.at[turn],
            device_id=(other // ny, lax.rem(other, ny)),
            device_id_type=MESH,
        )

    def iteration(turn, carry):
        norm_last, step_last = carry
        values = res[...].reshape(4, 3, cells, 128)
        grad_j, grad_k = derive_jk(values.reshape(12 * cells, 128))
        flux_j = (grad_j.reshape(4, 3, cells, 128) * cond[1][:, None]).reshape(12 * cells, 128)
        flux_k = (grad_k.reshape(4, 3, cells, 128) * cond[2][:, None]).reshape(12 * cells, 128)
        high, low = split(jnp.concatenate([flux_j, flux_k], axis=1))
        both = dot(high, bb_ref[...])
        stiff = both[:, :128] + both[:, 128:] + dot(low, bh_ref[...])
        stiff = stiff.reshape(4, 3, cells, 128)
        norm = jnp.zeros((cells, 128), f32)
        product = jnp.zeros((cells, 128), f32)
        for c in range(3):
            grads = derive_i([values[h, c] for h in range(4)], 0)
            fluxes = [grads[h] * cond[0, h] for h in range(4)]
            backs = derive_i(fluxes, 1)
            for h in range(4):
                here = values[h, c]
                applied = mass[h] * here + stiff[h, c] + backs[h]
                norm = norm + here * here * share[h]
                product = product + here * applied
                w[h, c] = applied.reshape(EX, EY, EZ, 128)
        norm = jnp.sum(norm, axis=0, keepdims=True)
        product = jnp.sum(product, axis=0, keepdims=True)
        sums[turn, me] = jnp.concatenate([norm, product], axis=0)

        def send(step, inner):
            sum_copy(turn, step).start()
            return inner

        lax.fori_loop(1, total, send, 0)

        @pl.when(turn < ITERS - 1)
        def _():
            fold_inside()
            send_faces(turn + 1)
            take_faces(turn + 1)
            sent_faces(turn + 1)

        arrived = sums.at[turn, pl.ds(0, total - 1)]
        pltpu.make_async_copy(arrived, arrived, sums_r.at[turn]).wait()
        gathered = jnp.sum(sums[turn], axis=0)
        totals = jnp.sum(gathered, axis=1, keepdims=True)
        norm = totals[0:1]
        product = totals[1:2]
        ratio = jnp.where(turn == 0, 0.0, norm / norm_last)
        step_len = norm / (product - ratio * norm / step_last)
        for h in range(4):
            moved = res[h] + ratio * dire[h]
            dire[h] = moved
            sol[h] = sol[h] + step_len * moved

            @pl.when(turn < ITERS - 1)
            def _():
                trail = w[h] + ratio * along[h]
                along[h] = trail
                res[h] = res[h] - step_len * trail

        pltpu.make_async_copy(arrived, arrived, sums_s.at[turn]).wait()
        return norm, step_len

    one = jnp.ones((1, 1), f32)
    lax.fori_loop(0, ITERS, iteration, (one, one))

    back = picks.T.astype(bf16)
    for c in range(3):
        parts = [sol[h, c].reshape(cells, 128) for h in range(4)]
        whole = jnp.concatenate(parts, axis=1)
        high, low = split(whole)
        third = (whole - high.astype(f32) - low.astype(f32)).astype(bf16)
        out_ref[c] = dot(back, high) + dot(back, low) + dot(back, third)


def local(nx, ny, adjoint_field, velocity, diffusivity, jacobian, element_slot):
    tables = [jnp.asarray(table) for table in constant_tables()]
    cells = element_slot.size
    nodes = adjoint_field.shape[-1]
    field = (4, 3, EX, EY, EZ, 128)
    vmem = pl.BlockSpec(memory_space=pltpu.VMEM)
    result = pl.pallas_call(
        functools.partial(kernel, nx, ny),
        out_shape=jax.ShapeDtypeStruct((3, cells, nodes), f32),
        in_specs=[vmem] * 11,
        out_specs=vmem,
        scratch_shapes=[
            pltpu.VMEM((4, cells, 128), f32),
            pltpu.VMEM((3, 4, cells, 128), f32),
            pltpu.VMEM((4, cells, 128), f32),
            pltpu.VMEM(field, f32),
            pltpu.VMEM(field, f32),
            pltpu.VMEM(field, f32),
            pltpu.VMEM(field, f32),
            pltpu.VMEM(field, f32),
            pltpu.VMEM((ITERS, 4, 3, EZ, 128), f32),
            pltpu.VMEM((ITERS, 4, 3, EZ, 128), f32),
            pltpu.VMEM((ITERS, 4, EZ, 128), f32),
            pltpu.VMEM((ITERS, 4, EZ, 128), f32),
            pltpu.VMEM((ITERS, nx * ny, 2, 128), f32),
            pltpu.SemaphoreType.DMA((ITERS, 4)),
            pltpu.SemaphoreType.DMA((ITERS, 4)),
            pltpu.SemaphoreType.DMA((ITERS, 4)),
            pltpu.SemaphoreType.DMA((ITERS, 4)),
            pltpu.SemaphoreType.DMA((ITERS,)),
            pltpu.SemaphoreType.DMA((ITERS,)),
        ],
        compiler_params=pltpu.CompilerParams(
            collective_id=0, has_side_effects=True, vmem_limit_bytes=48 * 1024 * 1024
        ),
    )(
        adjoint_field.reshape(3, cells, nodes),
        velocity.reshape(3, cells, nodes),
        diffusivity.reshape(3, cells, nodes),
        jacobian.reshape(1, cells, nodes),
        element_slot.reshape(1, cells),
        *tables,
    )
    return result.reshape(3, 1, 1, cells, nodes)


def solution(mesh):
    in_specs = (
        P(None, "gx", "gy", None, None),
        P(None, "gx", "gy", None, None),
        P(None, "gx", "gy", None, None),
        P("gx", "gy", None, None),
        P("gx", "gy", None),
    )
    out_specs = P(None, "gx", "gy", None, None)
    run = functools.partial(local, mesh.shape["gx"], mesh.shape["gy"])
    return jax.shard_map(run, mesh=mesh, in_specs=in_specs, out_specs=out_specs, check_vma=False)
```

```python
import functools

import jax
import jax.numpy as jnp
import numpy as np
from jax import lax
from jax.experimental import pallas as pl
from jax.experimental.pallas import tpu as pltpu
from jax.sharding import PartitionSpec as P

EX = 2
EY = 2
EZ = 16
ITERS = 4

time_step = 0.25
MESH = pl.DeviceIdType.MESH
f32 = jnp.float32
bf16 = jnp.bfloat16

SIDES = ((-1, 0), (1, 0), (0, -1), (0, 1))
CORNERS = ((-1, -1), (-1, 1), (1, -1), (1, 1))


def legendre_seven(points):
    previous = points * 0.0 + 1.0
    current = points
    for degree in range(1, 7):
        following = ((2 * degree + 1) * points * current - degree * previous) / (degree + 1)
        previous = current
        current = following
    return current


def gll_tables():
    poly_order = 7
    points = np.array(
        [
            -1.0,
            -0.8717401485096066,
            -0.5917001814331423,
            -0.2092992179024789,
            0.2092992179024789,
            0.5917001814331423,
            0.8717401485096066,
            1.0,
        ]
    )
    end_values = legendre_seven(points)
    weights = 2.0 / (poly_order * (poly_order + 1) * end_values**2)
    spread = points[:, None] - points[None, :]
    identity = np.eye(poly_order + 1)
    diff_table = end_values[:, None] / (end_values[None, :] * (spread + identity))
    diff_table = diff_table * (1.0 - identity)
    corners = np.zeros(poly_order + 1)
    corners[0] = -poly_order * (poly_order + 1) / 4.0
    corners[-1] = poly_order * (poly_order + 1) / 4.0
    diff_table = diff_table + identity * corners[None, :]
    return (weights.astype(np.float32), diff_table.astype(np.float32))


def constant_tables():
    weights, diff = gll_tables()
    eye = np.eye(8, dtype=np.float32)
    pair = np.eye(2, dtype=np.float32)
    along_j = np.kron(pair, np.kron(diff.T, eye))
    along_k = np.kron(pair, np.kron(eye, diff.T))
    coef = np.zeros((2, 2, 4, 4, 128), np.float32)
    for flip in range(2):
        matrix = diff.T if flip else diff
        for out in range(4):
            for inn in range(4):
                for il in range(2):
                    span = slice(il * 64, il * 64 + 64)
                    coef[flip, 0, out, inn, span] = matrix[2 * out + il, 2 * inn + il]
                    coef[flip, 1, out, inn, span] = matrix[2 * out + il, 2 * inn + 1 - il]
    coef = coef.reshape(64, 128)
    cube = weights[:, None, None] * weights[None, :, None] * weights[None, None, :]
    cube = np.concatenate([cube.reshape(4, 128), np.zeros((4, 128))])
    stack = [along_j, along_k, along_j.T, along_k.T, coef, cube]
    return np.concatenate(stack).astype(np.float32)


def dot(a, b):
    return jnp.dot(a, b, preferred_element_type=f32)


def split(values):
    high = values.astype(bf16)
    return high, (values - high.astype(f32)).astype(bf16)


def roll(values, shift, axis=None):
    axis = values.ndim - 1 if axis is None else axis
    shift = shift % values.shape[axis]
    return values if shift == 0 else pltpu.roll(values, shift, axis)


def kernel(
    nx,
    ny,
    adj_hbm,
    vel_hbm,
    dif_hbm,
    jac_hbm,
    slot_hbm,
    table_hbm,
    out_ref,
    adj_ref,
    vel_ref,
    dif_ref,
    jac_ref,
    slot_ref,
    table,
    forth,
    back,
    mass,
    cond,
    source,
    base0,
    base1,
    base2,
    base3,
    passed,
    dots,
    face_out,
    face_in,
    corner_out,
    corner_in,
    early_x,
    early_y,
    late,
    fetch_s,
    face_s,
    face_r,
    corner_s,
    corner_r,
    sums_s,
    sums_r,
):
    gx = lax.axis_index("gx")
    gy = lax.axis_index("gy")
    total = nx * ny
    me = gx * ny + gy
    cells = EX * EY * EZ

    fetches = [
        pltpu.make_async_copy(there, here, fetch_s.at[at])
        for at, (there, here) in enumerate(
            (
                (slot_hbm, slot_ref),
                (adj_hbm, adj_ref),
                (table_hbm, table),
                (jac_hbm, jac_ref),
                (vel_hbm, vel_ref),
                (dif_hbm, dif_ref),
            )
        )
    ]
    for fetch in fetches:
        fetch.start()
    got_slot, got_adj, got_table, got_jac, got_vel, got_dif = fetches

    face_in[...] = jnp.zeros_like(face_in)
    corner_in[...] = jnp.zeros_like(corner_in)

    barrier = pltpu.get_barrier_semaphore()

    def greet(step, carry):
        other = lax.rem(me + step, total)
        pl.semaphore_signal(
            barrier, inc=1, device_id=(other // ny, lax.rem(other, ny)), device_id_type=MESH
        )
        return carry

    lax.fori_loop(1, total, greet, 0)
    dots[...] = jnp.zeros_like(dots)

    lane = lax.broadcasted_iota(jnp.int32, (1, 128), 1)
    lane_j = (lane // 8) % 8
    lane_i = lane // 64
    group = lane // 8

    got_slot.wait()
    place = lax.broadcasted_iota(jnp.int32, (cells, cells), 0)
    picks = (jnp.broadcast_to(slot_ref[...], (cells, cells)) == place).astype(f32)
    pick = picks.astype(bf16)

    def thirds(values):
        high, low = split(values)
        return high, low, (values - high.astype(f32) - low.astype(f32)).astype(bf16)

    def to_brick(stored):
        high, low, last = thirds(stored)
        return dot(pick, high) + dot(pick, low) + dot(pick, last)

    def derive_jk(values):
        high, low = split(values)
        both = dot(jnp.concatenate([high, low], axis=1), forth[0:256, :])
        both = both + dot(high, forth[256:384, :])
        return both[:, :128], both[:, 128:]

    def derive_i(parts, flip):
        turned = [roll(part, 64) for part in parts]
        outs = []
        for out in range(4):
            acc = None
            for inn in range(4):
                at = 512 + flip * 32 + out * 4 + inn
                term = parts[inn] * table[at : at + 1, :]
                term = term + turned[inn] * table[at + 16 : at + 17, :]
                acc = term if acc is None else acc + term
            outs.append(acc)
        return outs

    def exists(side):
        ax, ay = gx + side[0], gy + side[1]
        return (ax >= 0) & (ax < nx) & (ay >= 0) & (ay < ny)

    def copies(turn, c):
        made = []
        groups = (
            (SIDES, face_out, face_in, face_s, face_r),
            (CORNERS, corner_out, corner_in, corner_s, corner_r),
        )
        for sides, outgoing, incoming, sent, received in groups:
            for d, side in enumerate(sides):
                copy = pltpu.make_async_remote_copy(
                    src_ref=outgoing.at[turn, c, d],
                    dst_ref=incoming.at[turn, c, d],
                    send_sem=sent.at[turn, c, d],
                    recv_sem=received.at[turn, c, d],
                    device_id=(gx + side[0], gy + side[1]),
                    device_id_type=MESH,
                )
                made.append((side, copy))
        return made

    def corner_spot(side):
        h = 0 if side[0] < 0 else 3
        x = 0 if side[0] < 0 else EX - 1
        y = 0 if side[1] < 0 else EY - 1
        start = (0 if side[0] < 0 else 64) + (0 if side[1] < 0 else 56)
        return h, x, y, start

    def fold_inside(values, dest, c):
        zed = lax.broadcasted_iota(jnp.int32, (EZ, 128), 0)
        kay = lax.broadcasted_iota(jnp.int32, (EZ, 128), 1) % 8
        upper = ((kay == 7) & (zed < EZ - 1)).astype(f32)
        lower = ((kay == 0) & (zed > 0)).astype(f32)
        flat = values.reshape(4 * cells, 128)
        stack = (4 * EX * EY, EZ, 128)
        from_next = roll(roll(flat, 7), -1, 0).reshape(stack)
        from_last = roll(roll(flat, -7), 1, 0).reshape(stack)
        summed = flat.reshape(stack) + from_next * upper[None] + from_last * lower[None]
        summed = summed.reshape(4, EX, EY, EZ, 128)
        columns = [summed[:, :, y] for y in range(EY)]
        folded = list(columns)
        for y in range(EY - 1):
            folded[y] = folded[y] + jnp.where(lane_j == 7, roll(columns[y + 1], 56), 0.0)
            folded[y + 1] = folded[y + 1] + jnp.where(lane_j == 0, roll(columns[y], -56), 0.0)
        for y in range(EY):
            dest[c, :, :, y] = folded[y]
        for x in range(EX - 1):
            left = dest[c, 3, x]
            right = dest[c, 0, x + 1]
            dest[c, 3, x] = left + jnp.where(lane_i == 1, roll(right, 64), 0.0)
            dest[c, 0, x + 1] = right + jnp.where(lane_i == 0, roll(left, 64), 0.0)

    def send_faces(turn, dest, c):
        left = dest[c, 0, 0]
        face_out[turn, c, 0] = jnp.where(lane_i == 0, left[0], roll(left[1], 64))
        right = dest[c, 3, EX - 1]
        face_out[turn, c, 1] = jnp.where(lane_i == 0, roll(right[0], 64), right[1])
        for d, y, j in ((2, 0, 0), (3, EY - 1, 7)):
            acc = None
            for h in range(4):
                for x in range(EX):
                    part = jnp.where(lane_j == j, dest[c, h, x, y], 0.0)
                    part = roll(part, h * 8 + x * 32 - j * 8)
                    acc = part if acc is None else acc + part
            face_out[turn, c, d] = acc
        for d, side in enumerate(CORNERS):
            h, x, y, start = corner_spot(side)
            corner_out[turn, c, d] = dest[c, h, x, y]
        for side, copy in copies(turn, c):
            pl.when(exists(side))(copy.start)

    def take_faces(turn, dest, c):
        for side, copy in copies(turn, c):
            pl.when(exists((-side[0], -side[1])))(copy.wait_recv)
        left = face_in[turn, c, 1]
        right = face_in[turn, c, 0]
        for h, x, arrived, here in ((0, 0, left, 0), (3, EX - 1, right, 1)):
            turned = roll(arrived, 64)
            pair = (arrived, turned) if here == 0 else (turned, arrived)
            for y in range(EY):
                dest[c, h, x, y] = dest[c, h, x, y] + jnp.where(lane_i == here, pair[y], 0.0)
        for d, y, j in ((3, 0, 0), (2, EY - 1, 7)):
            arrived = face_in[turn, c, d]
            for h in range(4):
                for x in range(EX):
                    part = roll(arrived, j * 8 - h * 8 - x * 32)
                    dest[c, h, x, y] = dest[c, h, x, y] + jnp.where(lane_j == j, part, 0.0)
        for d, side in enumerate(CORNERS):
            h, x, y, start = corner_spot((-side[0], -side[1]))
            other = corner_spot(side)[3]
            part = roll(corner_in[turn, c, d], start - other)
            dest[c, h, x, y] = dest[c, h, x, y] + jnp.where(group == start // 8, part, 0.0)

    def operate(values):
        grad_j, grad_k = derive_jk(values.reshape(4 * cells, 128))
        flux_j = grad_j * cond[1].reshape(4 * cells, 128)
        flux_k = grad_k * cond[2].reshape(4 * cells, 128)
        high, low = split(jnp.concatenate([flux_j, flux_k], axis=1))
        both = dot(high, back[...])
        stiff = both[:, :128] + both[:, 128:] + dot(low, back[:, 0:128])
        stiff = stiff.reshape(4, cells, 128)
        grads = derive_i([values[h] for h in range(4)], 0)
        fluxes = [grads[h] * cond[0, h] for h in range(4)]
        backs = derive_i(fluxes, 1)
        return [mass[h] * values[h] + stiff[h] + backs[h] for h in range(4)]

    def load(ref, c):
        return ref[c].reshape(4, cells, 128)

    def add_dot(at, first, second):
        acc = dots[at]
        for h in range(4):
            acc = acc + jnp.sum((first[h] * second[h]).reshape(cells // 8, 8, 128), axis=0)
        dots[at] = acc

    def in_row(first, last):
        sums = jnp.sum(jnp.sum(dots[first:last], axis=1), axis=1, keepdims=True)
        spot = lax.broadcasted_iota(jnp.int32, (last - first, 128), 0)
        here = lax.broadcasted_iota(jnp.int32, (last - first, 128), 1)
        return jnp.sum(jnp.where(spot == here, sums, 0.0), axis=0, keepdims=True)

    def spread_sums(buffer, at, spot, count, device):
        buffer[spot] = buffer_row[0]

        def send(step, carry):
            pltpu.make_async_remote_copy(
                src_ref=buffer.at[spot],
                dst_ref=buffer.at[spot],
                send_sem=sums_s.at[at],
                recv_sem=sums_r.at[at],
                device_id=device(step),
                device_id_type=MESH,
            ).start()
            return carry

        lax.fori_loop(1, count, send, 0)

    def await_sums(buffer, at, count, sems):
        arrived = buffer.at[pl.ds(0, count - 1)]
        pltpu.make_async_copy(arrived, arrived, sems.at[at]).wait()

    buffer_row = [None]

    def along_x(step):
        return lax.rem(gx + step, nx), gy

    def along_y(step):
        return gx, lax.rem(gy + step, ny)

    def anywhere(step):
        other = lax.rem(me + step, total)
        return other // ny, lax.rem(other, ny)

    got_adj.wait()
    adj = [to_brick(adj_ref[c]) for c in range(3)]
    got_table.wait()
    f_high, f_low = split(jnp.concatenate([table[0:128], table[128:256]], axis=1))
    forth[0:128, :] = f_high
    forth[128:256, :] = f_high
    forth[256:384, :] = f_low
    b_high, b_low = split(table[256:512])
    back[...] = jnp.concatenate([b_high, b_low], axis=1)
    got_jac.wait()
    jac = to_brick(jac_ref[0])
    for h in range(4):
        mass[h] = jac[:, h * 128 : h * 128 + 128] * table[576 + h : 577 + h, :]
    full = [[adj[c][:, h * 128 : h * 128 + 128] for h in range(4)] for c in range(3)]
    grad_j, grad_k, grad_i = [], [], []
    for c in range(3):
        g_j, g_k = derive_jk(jnp.concatenate(full[c], axis=0))
        grad_j.append(g_j.reshape(4, cells, 128))
        grad_k.append(g_k.reshape(4, cells, 128))
        grad_i.append(derive_i(full[c], 0))
    got_vel.wait()
    flow = [dot(pick, vel_ref[c]) for c in range(3)]
    for h in range(4):
        at = slice(h * 128, h * 128 + 128)
        v = [flow[c][:, at] for c in range(3)]
        r = [
            grad_j[2][h] - grad_k[1][h],
            grad_k[0][h] - grad_i[2][h],
            grad_i[1][h] - grad_j[0][h],
        ]
        for c in range(3):
            c1, c2 = (c + 1) % 3, (c + 2) % 3
            value = full[c][h] + time_step * (v[c1] * r[c2] - v[c2] * r[c1])
            source[c, h] = mass[h] * value

    pl.semaphore_wait(barrier, total - 1)

    def first_send(c, carry):
        fold_inside(source[c], base0, c)
        send_faces(0, base0, c)
        return carry

    lax.fori_loop(0, 3, first_send, 0)

    got_dif.wait()
    for m in range(3):
        con = to_brick(dif_ref[m])
        for h in range(4):
            weight = time_step * table[576 + h : 577 + h, :]
            cond[m, h] = con[:, h * 128 : h * 128 + 128] * weight

    def turn_0(c, carry):
        take_faces(0, base0, c)
        values = load(base0, c)
        add_dot(0, values, source[c])
        applied = operate(values)
        add_dot(1, values, applied)
        fold_inside(jnp.stack(applied), base1, c)
        send_faces(1, base1, c)
        return carry

    lax.fori_loop(0, 3, turn_0, 0)
    buffer_row[0] = in_row(0, 8)
    spread_sums(early_x, 0, gx, nx, along_x)

    def turn_1(c, carry):
        @pl.when(c == 1)
        def _():
            await_sums(early_x, 0, nx, sums_r)
            buffer_row[0] = jnp.sum(early_x[...], axis=0)
            spread_sums(early_y, 1, gy, ny, along_y)

        take_faces(1, base1, c)
        values = load(base1, c)
        applied = operate(values)
        add_dot(8, load(base0, c), applied)
        add_dot(9, values, applied)
        fold_inside(jnp.stack(applied), passed, c)
        send_faces(2, passed, c)
        return carry

    lax.fori_loop(0, 3, turn_1, 0)
    await_sums(early_y, 1, ny, sums_r)
    early = jnp.sum(early_y[...], axis=0)
    norm = early[:, 0:1]
    first = early[:, 1:2]
    inv = norm / (1.75 * first)

    def turn_2(c, carry):
        take_faces(2, passed, c)
        u0, u1, q = load(base0, c), load(base1, c), load(passed, c)
        v1 = inv * u1 - u0
        values = 2.0 * (inv * (inv * q - u1) - v1) - u0
        base2[c] = values
        applied = operate(values)
        add_dot(10, u0, applied)
        add_dot(11, u1, applied)
        add_dot(12, values, applied)
        fold_inside(jnp.stack(applied), passed, c)
        send_faces(3, passed, c)
        return carry

    lax.fori_loop(0, 3, turn_2, 0)

    def turn_3(c, carry):
        take_faces(3, passed, c)
        u0, u1, v2, q = load(base0, c), load(base1, c), base2[c], load(passed, c)
        values = 2.0 * (inv * q - v2) - (inv * u1 - u0)
        base3[c] = values
        applied = operate(values)
        add_dot(13, u0, applied)
        add_dot(14, u1, applied)
        add_dot(15, v2, applied)
        add_dot(16, values, applied)
        return carry

    lax.fori_loop(0, 3, turn_3, 0)
    buffer_row[0] = in_row(8, 24)
    spread_sums(late, 2, me, total, anywhere)

    def drain(at, carry):
        for side, copy in copies(at // 3, at % 3):
            pl.when(exists(side))(copy.wait_send)
        return carry

    lax.fori_loop(0, 3 * ITERS, drain, 0)
    await_sums(early_x, 0, nx, sums_s)
    await_sums(early_y, 1, ny, sums_s)

    await_sums(late, 2, total, sums_r)
    row = jnp.sum(late[...], axis=0)
    d = [row[:, at : at + 1] for at in range(9)]
    a = inv * first
    g2 = 2.0 * inv * inv * d[0] - 4.0 * a + norm
    g3 = 2.0 * (inv * d[2] - g2) - (a - norm)
    gram = [
        [first, d[0], d[2], d[5]],
        [d[0], d[1], d[3], d[6]],
        [d[2], d[3], d[4], d[7]],
        [d[5], d[6], d[7], d[8]],
    ]
    side = [norm, first, g2, g3]
    diagonal = [gram[at][at] for at in range(4)]
    inverse = []
    for at in range(4):
        pivot = gram[at][at]
        usable = pivot > 1e-6 * diagonal[at]
        inverse.append(jnp.where(usable, 1.0 / pivot, 0.0))
        for below in range(at + 1, 4):
            factor = gram[below][at] * inverse[at]
            for across in range(at + 1, 4):
                gram[below][across] = gram[below][across] - factor * gram[at][across]
            side[below] = side[below] - factor * side[at]
    weights = [None] * 4
    for at in (3, 2, 1, 0):
        value = side[at]
        for across in range(at + 1, 4):
            value = value - gram[at][across] * weights[across]
        weights[at] = value * inverse[at]

    put_back = picks.T.astype(bf16)
    for c in range(3):
        mixed = weights[0] * load(base0, c) + weights[1] * load(base1, c)
        mixed = mixed + weights[2] * base2[c] + weights[3] * base3[c]
        whole = jnp.concatenate([mixed[h] for h in range(4)], axis=1)
        high, low, last = thirds(whole)
        out_ref[c] = dot(put_back, high) + dot(put_back, low) + dot(put_back, last)
    await_sums(late, 2, total, sums_s)


def local(nx, ny, adjoint_field, velocity, diffusivity, jacobian, element_slot):
    table = jnp.asarray(constant_tables())
    cells = element_slot.size
    nodes = adjoint_field.shape[-1]
    brick = (3, 4, EX, EY, EZ, 128)
    flat = (3, 4, cells, 128)
    hbm = pl.BlockSpec(memory_space=pltpu.HBM)
    result = pl.pallas_call(
        functools.partial(kernel, nx, ny),
        out_shape=jax.ShapeDtypeStruct((3, cells, nodes), f32),
        in_specs=[hbm] * 6,
        out_specs=pl.BlockSpec(memory_space=pltpu.VMEM),
        scratch_shapes=[
            pltpu.VMEM((3, cells, nodes), f32),
            pltpu.VMEM((3, cells, nodes), bf16),
            pltpu.VMEM((3, cells, nodes), f32),
            pltpu.VMEM((1, cells, nodes), f32),
            pltpu.VMEM((1, cells), jnp.int32),
            pltpu.VMEM(table.shape, f32),
            pltpu.VMEM((384, 256), bf16),
            pltpu.VMEM((256, 256), bf16),
            pltpu.VMEM((4, cells, 128), f32),
            pltpu.VMEM(flat, f32),
            pltpu.VMEM(flat, f32),
            pltpu.VMEM(brick, f32),
            pltpu.VMEM(brick, f32),
            pltpu.VMEM(flat, f32),
            pltpu.VMEM(flat, f32),
            pltpu.VMEM(brick, f32),
            pltpu.VMEM((24, 8, 128), f32),
            pltpu.VMEM((ITERS, 3, 4, EZ, 128), f32),
            pltpu.VMEM((ITERS, 3, 4, EZ, 128), f32),
            pltpu.VMEM((ITERS, 3, 4, EZ, 128), f32),
            pltpu.VMEM((ITERS, 3, 4, EZ, 128), f32),
            pltpu.VMEM((nx, 1, 128), f32),
            pltpu.VMEM((ny, 1, 128), f32),
            pltpu.VMEM((nx * ny, 1, 128), f32),
            pltpu.SemaphoreType.DMA((6,)),
            pltpu.SemaphoreType.DMA((ITERS, 3, 4)),
            pltpu.SemaphoreType.DMA((ITERS, 3, 4)),
            pltpu.SemaphoreType.DMA((ITERS, 3, 4)),
            pltpu.SemaphoreType.DMA((ITERS, 3, 4)),
            pltpu.SemaphoreType.DMA((3,)),
            pltpu.SemaphoreType.DMA((3,)),
        ],
        compiler_params=pltpu.CompilerParams(
            collective_id=0, has_side_effects=True, vmem_limit_bytes=48 * 1024 * 1024
        ),
    )(
        adjoint_field.reshape(3, cells, nodes),
        velocity.reshape(3, cells, nodes),
        diffusivity.reshape(3, cells, nodes),
        jacobian.reshape(1, cells, nodes),
        element_slot.reshape(1, cells),
        table,
    )
    return result.reshape(3, 1, 1, cells, nodes)


def solution(mesh):
    in_specs = (
        P(None, "gx", "gy", None, None),
        P(None, "gx", "gy", None, None),
        P(None, "gx", "gy", None, None),
        P("gx", "gy", None, None),
        P("gx", "gy", None),
    )
    out_specs = P(None, "gx", "gy", None, None)
    run = functools.partial(local, mesh.shape["gx"], mesh.shape["gy"])
    return jax.shard_map(run, mesh=mesh, in_specs=in_specs, out_specs=out_specs, check_vma=False)
```

```python
import functools

import jax
import jax.numpy as jnp
import numpy as np
from jax import lax
from jax.experimental import pallas as pl
from jax.experimental.pallas import tpu as pltpu
from jax.sharding import PartitionSpec as P

EX = 2
EY = 2
EZ = 16
ITERS = 4

time_step = 0.25
MESH = pl.DeviceIdType.MESH
f32 = jnp.float32
bf16 = jnp.bfloat16

SIDES = ((-1, 0), (1, 0), (0, -1), (0, 1))
CORNERS = ((-1, -1), (-1, 1), (1, -1), (1, 1))


def legendre_seven(points):
    previous = points * 0.0 + 1.0
    current = points
    for degree in range(1, 7):
        following = ((2 * degree + 1) * points * current - degree * previous) / (degree + 1)
        previous = current
        current = following
    return current


def gll_tables():
    poly_order = 7
    points = np.array(
        [
            -1.0,
            -0.8717401485096066,
            -0.5917001814331423,
            -0.2092992179024789,
            0.2092992179024789,
            0.5917001814331423,
            0.8717401485096066,
            1.0,
        ]
    )
    end_values = legendre_seven(points)
    weights = 2.0 / (poly_order * (poly_order + 1) * end_values**2)
    spread = points[:, None] - points[None, :]
    identity = np.eye(poly_order + 1)
    diff_table = end_values[:, None] / (end_values[None, :] * (spread + identity))
    diff_table = diff_table * (1.0 - identity)
    corners = np.zeros(poly_order + 1)
    corners[0] = -poly_order * (poly_order + 1) / 4.0
    corners[-1] = poly_order * (poly_order + 1) / 4.0
    diff_table = diff_table + identity * corners[None, :]
    return (weights.astype(np.float32), diff_table.astype(np.float32))


def constant_tables():
    weights, diff = gll_tables()
    eye = np.eye(8, dtype=np.float32)
    pair = np.eye(2, dtype=np.float32)
    along_j = np.kron(pair, np.kron(diff.T, eye))
    along_k = np.kron(pair, np.kron(eye, diff.T))
    coef = np.zeros((2, 2, 4, 4, 128), np.float32)
    for flip in range(2):
        matrix = diff.T if flip else diff
        for out in range(4):
            for inn in range(4):
                for il in range(2):
                    span = slice(il * 64, il * 64 + 64)
                    coef[flip, 0, out, inn, span] = matrix[2 * out + il, 2 * inn + il]
                    coef[flip, 1, out, inn, span] = matrix[2 * out + il, 2 * inn + 1 - il]
    coef = coef.reshape(64, 128)
    cube = weights[:, None, None] * weights[None, :, None] * weights[None, None, :]
    cube = np.concatenate([cube.reshape(4, 128), np.zeros((4, 128))])
    stack = [along_j, along_k, along_j.T, along_k.T, coef, cube]
    return np.concatenate(stack).astype(np.float32)


def dot(a, b):
    return jnp.dot(a, b, preferred_element_type=f32)


def split(values):
    high = values.astype(bf16)
    return high, (values - high.astype(f32)).astype(bf16)


def roll(values, shift, axis=None):
    axis = values.ndim - 1 if axis is None else axis
    shift = shift % values.shape[axis]
    return values if shift == 0 else pltpu.roll(values, shift, axis)


def kernel(
    nx,
    ny,
    adj_hbm,
    vel_hbm,
    dif_hbm,
    jac_hbm,
    slot_hbm,
    table_hbm,
    out_ref,
    adj_ref,
    vel_ref,
    dif_ref,
    jac_ref,
    slot_ref,
    table,
    forth,
    back,
    mass,
    cond,
    source,
    base0,
    base1,
    base2,
    base3,
    passed,
    dots,
    face_out,
    face_in,
    corner_out,
    corner_in,
    early_x,
    early_y,
    late,
    fetch_s,
    face_s,
    face_r,
    corner_s,
    corner_r,
    sums_s,
    sums_r,
):
    gx = lax.axis_index("gx")
    gy = lax.axis_index("gy")
    total = nx * ny
    me = gx * ny + gy
    cells = EX * EY * EZ

    fetches = [
        pltpu.make_async_copy(there, here, fetch_s.at[at])
        for at, (there, here) in enumerate(
            (
                (slot_hbm, slot_ref),
                (adj_hbm, adj_ref),
                (table_hbm, table),
                (jac_hbm, jac_ref),
                (vel_hbm, vel_ref),
                (dif_hbm, dif_ref),
            )
        )
    ]
    for fetch in fetches:
        fetch.start()
    got_slot, got_adj, got_table, got_jac, got_vel, got_dif = fetches

    face_in[...] = jnp.zeros_like(face_in)
    corner_in[...] = jnp.zeros_like(corner_in)

    barrier = pltpu.get_barrier_semaphore()

    def greet(step, carry):
        other = lax.rem(me + step, total)
        pl.semaphore_signal(
            barrier, inc=1, device_id=(other // ny, lax.rem(other, ny)), device_id_type=MESH
        )
        return carry

    lax.fori_loop(1, total, greet, 0)
    dots[...] = jnp.zeros_like(dots)

    lane = lax.broadcasted_iota(jnp.int32, (1, 128), 1)
    lane_j = (lane // 8) % 8
    lane_i = lane // 64
    group = lane // 8

    got_slot.wait()
    place = lax.broadcasted_iota(jnp.int32, (cells, cells), 0)
    picks = (jnp.broadcast_to(slot_ref[...], (cells, cells)) == place).astype(f32)
    pick = picks.astype(bf16)

    pick_both = jnp.concatenate([pick, pick], axis=1)

    def to_brick(stored):
        return dot(pick_both, jnp.concatenate(split(stored), axis=0))

    def derive_jk(values):
        high, low = split(values)
        both = dot(jnp.concatenate([high, low], axis=1), forth[0:256, :])
        both = both + dot(high, forth[256:384, :])
        return both[:, :128], both[:, 128:]

    def derive_i(parts, flip):
        turned = [roll(part, 64) for part in parts]
        outs = []
        for out in range(4):
            acc = None
            for inn in range(4):
                at = 512 + flip * 32 + out * 4 + inn
                term = parts[inn] * table[at : at + 1, :]
                term = term + turned[inn] * table[at + 16 : at + 17, :]
                acc = term if acc is None else acc + term
            outs.append(acc)
        return outs

    def exists(side):
        ax, ay = gx + side[0], gy + side[1]
        return (ax >= 0) & (ax < nx) & (ay >= 0) & (ay < ny)

    def copies(turn, c):
        made = []
        groups = (
            (SIDES, face_out, face_in, face_s, face_r),
            (CORNERS, corner_out, corner_in, corner_s, corner_r),
        )
        for sides, outgoing, incoming, sent, received in groups:
            for d, side in enumerate(sides):
                copy = pltpu.make_async_remote_copy(
                    src_ref=outgoing.at[turn, c, d],
                    dst_ref=incoming.at[turn, c, d],
                    send_sem=sent.at[turn, c, d],
                    recv_sem=received.at[turn, c, d],
                    device_id=(gx + side[0], gy + side[1]),
                    device_id_type=MESH,
                )
                made.append((side, copy))
        return made

    def corner_spot(side):
        h = 0 if side[0] < 0 else 3
        x = 0 if side[0] < 0 else EX - 1
        y = 0 if side[1] < 0 else EY - 1
        start = (0 if side[0] < 0 else 64) + (0 if side[1] < 0 else 56)
        return h, x, y, start

    def fold_inside(values, dest, c):
        zed = lax.broadcasted_iota(jnp.int32, (EZ, 128), 0)
        kay = lax.broadcasted_iota(jnp.int32, (EZ, 128), 1) % 8
        upper = ((kay == 7) & (zed < EZ - 1)).astype(f32)
        lower = ((kay == 0) & (zed > 0)).astype(f32)
        flat = values.reshape(4 * cells, 128)
        stack = (4 * EX * EY, EZ, 128)
        from_next = roll(roll(flat, 7), -1, 0).reshape(stack)
        from_last = roll(roll(flat, -7), 1, 0).reshape(stack)
        summed = flat.reshape(stack) + from_next * upper[None] + from_last * lower[None]
        summed = summed.reshape(4, EX, EY, EZ, 128)
        columns = [summed[:, :, y] for y in range(EY)]
        folded = list(columns)
        for y in range(EY - 1):
            folded[y] = folded[y] + jnp.where(lane_j == 7, roll(columns[y + 1], 56), 0.0)
            folded[y + 1] = folded[y + 1] + jnp.where(lane_j == 0, roll(columns[y], -56), 0.0)
        for y in range(EY):
            dest[c, :, :, y] = folded[y]
        for x in range(EX - 1):
            left = dest[c, 3, x]
            right = dest[c, 0, x + 1]
            dest[c, 3, x] = left + jnp.where(lane_i == 1, roll(right, 64), 0.0)
            dest[c, 0, x + 1] = right + jnp.where(lane_i == 0, roll(left, 64), 0.0)

    def send_faces(turn, dest, c):
        left = dest[c, 0, 0]
        face_out[turn, c, 0] = jnp.where(lane_i == 0, left[0], roll(left[1], 64))
        right = dest[c, 3, EX - 1]
        face_out[turn, c, 1] = jnp.where(lane_i == 0, roll(right[0], 64), right[1])
        for d, y, j in ((2, 0, 0), (3, EY - 1, 7)):
            acc = None
            for h in range(4):
                for x in range(EX):
                    part = jnp.where(lane_j == j, dest[c, h, x, y], 0.0)
                    part = roll(part, h * 8 + x * 32 - j * 8)
                    acc = part if acc is None else acc + part
            face_out[turn, c, d] = acc
        for d, side in enumerate(CORNERS):
            h, x, y, start = corner_spot(side)
            corner_out[turn, c, d] = dest[c, h, x, y]
        for side, copy in copies(turn, c):
            pl.when(exists(side))(copy.start)

    def take_faces(turn, dest, c):
        for side, copy in copies(turn, c):
            pl.when(exists((-side[0], -side[1])))(copy.wait_recv)
        left = face_in[turn, c, 1]
        right = face_in[turn, c, 0]
        for h, x, arrived, here in ((0, 0, left, 0), (3, EX - 1, right, 1)):
            turned = roll(arrived, 64)
            pair = (arrived, turned) if here == 0 else (turned, arrived)
            for y in range(EY):
                dest[c, h, x, y] = dest[c, h, x, y] + jnp.where(lane_i == here, pair[y], 0.0)
        for d, y, j in ((3, 0, 0), (2, EY - 1, 7)):
            arrived = face_in[turn, c, d]
            for h in range(4):
                for x in range(EX):
                    part = roll(arrived, j * 8 - h * 8 - x * 32)
                    dest[c, h, x, y] = dest[c, h, x, y] + jnp.where(lane_j == j, part, 0.0)
        for d, side in enumerate(CORNERS):
            h, x, y, start = corner_spot((-side[0], -side[1]))
            other = corner_spot(side)[3]
            part = roll(corner_in[turn, c, d], start - other)
            dest[c, h, x, y] = dest[c, h, x, y] + jnp.where(group == start // 8, part, 0.0)

    def operate(values):
        grad_j, grad_k = derive_jk(values.reshape(4 * cells, 128))
        flux_j = grad_j * cond[1].reshape(4 * cells, 128)
        flux_k = grad_k * cond[2].reshape(4 * cells, 128)
        high, low = split(jnp.concatenate([flux_j, flux_k], axis=1))
        both = dot(high, back[...])
        stiff = both[:, :128] + both[:, 128:] + dot(low, back[:, 0:128])
        stiff = stiff.reshape(4, cells, 128)
        grads = derive_i([values[h] for h in range(4)], 0)
        fluxes = [grads[h] * cond[0, h] for h in range(4)]
        backs = derive_i(fluxes, 1)
        return [mass[h] * values[h] + stiff[h] + backs[h] for h in range(4)]

    def load(ref, c):
        return ref[c].reshape(4, cells, 128)

    def add_dot(at, first, second):
        acc = dots[at]
        for h in range(4):
            acc = acc + jnp.sum((first[h] * second[h]).reshape(cells // 8, 8, 128), axis=0)
        dots[at] = acc

    def in_row(first, last):
        sums = jnp.sum(jnp.sum(dots[first:last], axis=1), axis=1, keepdims=True)
        spot = lax.broadcasted_iota(jnp.int32, (last - first, 128), 0)
        here = lax.broadcasted_iota(jnp.int32, (last - first, 128), 1)
        return jnp.sum(jnp.where(spot == here, sums, 0.0), axis=0, keepdims=True)

    def spread_sums(row, buffer, at, spot, count, device):
        buffer[spot] = row

        def send(step, carry):
            pltpu.make_async_remote_copy(
                src_ref=buffer.at[spot],
                dst_ref=buffer.at[spot],
                send_sem=sums_s.at[at],
                recv_sem=sums_r.at[at],
                device_id=device(step),
                device_id_type=MESH,
            ).start()
            return carry

        lax.fori_loop(1, count, send, 0)

    def await_sums(buffer, at, count, sems):
        arrived = buffer.at[pl.ds(0, count - 1)]
        pltpu.make_async_copy(arrived, arrived, sems.at[at]).wait()

    def along_x(step):
        return lax.rem(gx + step, nx), gy

    def along_y(step):
        return gx, lax.rem(gy + step, ny)

    def anywhere(step):
        other = lax.rem(me + step, total)
        return other // ny, lax.rem(other, ny)

    got_adj.wait()
    adj = [to_brick(adj_ref[c]) for c in range(3)]
    got_table.wait()
    f_high, f_low = split(jnp.concatenate([table[0:128], table[128:256]], axis=1))
    forth[0:128, :] = f_high
    forth[128:256, :] = f_high
    forth[256:384, :] = f_low
    b_high, b_low = split(table[256:512])
    back[...] = jnp.concatenate([b_high, b_low], axis=1)
    got_jac.wait()
    jac = to_brick(jac_ref[0])
    for h in range(4):
        mass[h] = jac[:, h * 128 : h * 128 + 128] * table[576 + h : 577 + h, :]
    full = [[adj[c][:, h * 128 : h * 128 + 128] for h in range(4)] for c in range(3)]
    grad_j, grad_k, grad_i = [], [], []
    for c in range(3):
        g_j, g_k = derive_jk(jnp.concatenate(full[c], axis=0))
        grad_j.append(g_j.reshape(4, cells, 128))
        grad_k.append(g_k.reshape(4, cells, 128))
        grad_i.append(derive_i(full[c], 0))
    got_vel.wait()
    flow = [dot(pick, vel_ref[c]) for c in range(3)]
    for h in range(4):
        at = slice(h * 128, h * 128 + 128)
        v = [flow[c][:, at] for c in range(3)]
        r = [
            grad_j[2][h] - grad_k[1][h],
            grad_k[0][h] - grad_i[2][h],
            grad_i[1][h] - grad_j[0][h],
        ]
        for c in range(3):
            c1, c2 = (c + 1) % 3, (c + 2) % 3
            value = full[c][h] + time_step * (v[c1] * r[c2] - v[c2] * r[c1])
            source[c, h] = mass[h] * value

    pl.semaphore_wait(barrier, total - 1)

    def first_send(c, carry):
        fold_inside(source[c], base0, c)
        send_faces(0, base0, c)
        return carry

    lax.fori_loop(0, 3, first_send, 0)

    got_dif.wait()
    for m in range(3):
        con = to_brick(dif_ref[m])
        for h in range(4):
            weight = time_step * table[576 + h : 577 + h, :]
            cond[m, h] = con[:, h * 128 : h * 128 + 128] * weight

    def turn_0(c, carry):
        take_faces(0, base0, c)
        values = load(base0, c)
        add_dot(0, values, source[c])
        applied = operate(values)
        add_dot(1, values, applied)
        fold_inside(jnp.stack(applied), base1, c)
        send_faces(1, base1, c)
        return carry

    lax.fori_loop(0, 3, turn_0, 0)
    spread_sums(in_row(0, 8), early_x, 0, gx, nx, along_x)

    def turn_1(c, carry):
        @pl.when(c == 1)
        def _():
            await_sums(early_x, 0, nx, sums_r)
            spread_sums(jnp.sum(early_x[...], axis=0), early_y, 1, gy, ny, along_y)

        take_faces(1, base1, c)
        values = load(base1, c)
        applied = operate(values)
        add_dot(8, load(base0, c), applied)
        add_dot(9, values, applied)
        fold_inside(jnp.stack(applied), passed, c)
        send_faces(2, passed, c)
        return carry

    lax.fori_loop(0, 3, turn_1, 0)
    await_sums(early_y, 1, ny, sums_r)
    early = jnp.sum(early_y[...], axis=0)
    norm = early[:, 0:1]
    first = early[:, 1:2]
    inv = norm / (1.75 * first)

    def turn_2(c, carry):
        take_faces(2, passed, c)
        u0, u1, q = load(base0, c), load(base1, c), load(passed, c)
        v1 = inv * u1 - u0
        values = 2.0 * (inv * (inv * q - u1) - v1) - u0
        base2[c] = values
        applied = operate(values)
        add_dot(10, u0, applied)
        add_dot(11, u1, applied)
        add_dot(12, values, applied)
        fold_inside(jnp.stack(applied), passed, c)
        send_faces(3, passed, c)
        return carry

    lax.fori_loop(0, 3, turn_2, 0)

    def turn_3(c, carry):
        take_faces(3, passed, c)
        u0, u1, v2, q = load(base0, c), load(base1, c), base2[c], load(passed, c)
        values = 2.0 * (inv * q - v2) - (inv * u1 - u0)
        base3[c] = values
        applied = operate(values)
        add_dot(13, u0, applied)
        add_dot(14, u1, applied)
        add_dot(15, v2, applied)
        add_dot(16, values, applied)
        return carry

    lax.fori_loop(0, 3, turn_3, 0)
    spread_sums(in_row(8, 24), late, 2, me, total, anywhere)

    def drain(at, carry):
        for side, copy in copies(at // 3, at % 3):
            pl.when(exists(side))(copy.wait_send)
        return carry

    lax.fori_loop(0, 3 * ITERS, drain, 0)
    await_sums(early_x, 0, nx, sums_s)
    await_sums(early_y, 1, ny, sums_s)

    await_sums(late, 2, total, sums_r)
    row = jnp.sum(late[...], axis=0)
    d = [row[:, at : at + 1] for at in range(9)]
    a = inv * first
    g2 = 2.0 * inv * inv * d[0] - 4.0 * a + norm
    g3 = 2.0 * (inv * d[2] - g2) - (a - norm)
    gram = [
        [first, d[0], d[2], d[5]],
        [d[0], d[1], d[3], d[6]],
        [d[2], d[3], d[4], d[7]],
        [d[5], d[6], d[7], d[8]],
    ]
    side = [norm, first, g2, g3]
    diagonal = [gram[at][at] for at in range(4)]
    inverse = []
    for at in range(4):
        pivot = gram[at][at]
        usable = pivot > 1e-6 * diagonal[at]
        inverse.append(jnp.where(usable, 1.0 / pivot, 0.0))
        for below in range(at + 1, 4):
            factor = gram[below][at] * inverse[at]
            for across in range(at + 1, 4):
                gram[below][across] = gram[below][across] - factor * gram[at][across]
            side[below] = side[below] - factor * side[at]
    weights = [None] * 4
    for at in (3, 2, 1, 0):
        value = side[at]
        for across in range(at + 1, 4):
            value = value - gram[at][across] * weights[across]
        weights[at] = value * inverse[at]

    put_back = picks.T.astype(bf16)
    put_back = jnp.concatenate([put_back, put_back], axis=1)
    for c in range(3):
        mixed = weights[0] * load(base0, c) + weights[1] * load(base1, c)
        mixed = mixed + weights[2] * base2[c] + weights[3] * base3[c]
        whole = jnp.concatenate([mixed[h] for h in range(4)], axis=1)
        out_ref[c] = dot(put_back, jnp.concatenate(split(whole), axis=0))
    await_sums(late, 2, total, sums_s)


def local(nx, ny, adjoint_field, velocity, diffusivity, jacobian, element_slot):
    table = jnp.asarray(constant_tables())
    cells = element_slot.size
    nodes = adjoint_field.shape[-1]
    brick = (3, 4, EX, EY, EZ, 128)
    flat = (3, 4, cells, 128)
    hbm = pl.BlockSpec(memory_space=pltpu.HBM)
    result = pl.pallas_call(
        functools.partial(kernel, nx, ny),
        out_shape=jax.ShapeDtypeStruct((3, cells, nodes), f32),
        in_specs=[hbm] * 6,
        out_specs=pl.BlockSpec(memory_space=pltpu.VMEM),
        scratch_shapes=[
            pltpu.VMEM((3, cells, nodes), f32),
            pltpu.VMEM((3, cells, nodes), bf16),
            pltpu.VMEM((3, cells, nodes), f32),
            pltpu.VMEM((1, cells, nodes), f32),
            pltpu.VMEM((1, cells), jnp.int32),
            pltpu.VMEM(table.shape, f32),
            pltpu.VMEM((384, 256), bf16),
            pltpu.VMEM((256, 256), bf16),
            pltpu.VMEM((4, cells, 128), f32),
            pltpu.VMEM(flat, f32),
            pltpu.VMEM(flat, f32),
            pltpu.VMEM(brick, f32),
            pltpu.VMEM(brick, f32),
            pltpu.VMEM(flat, f32),
            pltpu.VMEM(flat, f32),
            pltpu.VMEM(brick, f32),
            pltpu.VMEM((24, 8, 128), f32),
            pltpu.VMEM((ITERS, 3, 4, EZ, 128), f32),
            pltpu.VMEM((ITERS, 3, 4, EZ, 128), f32),
            pltpu.VMEM((ITERS, 3, 4, EZ, 128), f32),
            pltpu.VMEM((ITERS, 3, 4, EZ, 128), f32),
            pltpu.VMEM((nx, 1, 128), f32),
            pltpu.VMEM((ny, 1, 128), f32),
            pltpu.VMEM((nx * ny, 1, 128), f32),
            pltpu.SemaphoreType.DMA((6,)),
            pltpu.SemaphoreType.DMA((ITERS, 3, 4)),
            pltpu.SemaphoreType.DMA((ITERS, 3, 4)),
            pltpu.SemaphoreType.DMA((ITERS, 3, 4)),
            pltpu.SemaphoreType.DMA((ITERS, 3, 4)),
            pltpu.SemaphoreType.DMA((3,)),
            pltpu.SemaphoreType.DMA((3,)),
        ],
        compiler_params=pltpu.CompilerParams(
            collective_id=0, has_side_effects=True
        ),
    )(
        adjoint_field.reshape(3, cells, nodes),
        velocity.reshape(3, cells, nodes),
        diffusivity.reshape(3, cells, nodes),
        jacobian.reshape(1, cells, nodes),
        element_slot.reshape(1, cells),
        table,
    )
    return result.reshape(3, 1, 1, cells, nodes)


def solution(mesh):
    in_specs = (
        P(None, "gx", "gy", None, None),
        P(None, "gx", "gy", None, None),
        P(None, "gx", "gy", None, None),
        P("gx", "gy", None, None),
        P("gx", "gy", None),
    )
    out_specs = P(None, "gx", "gy", None, None)
    run = functools.partial(local, mesh.shape["gx"], mesh.shape["gy"])
    return jax.shard_map(run, mesh=mesh, in_specs=in_specs, out_specs=out_specs, check_vma=False)
```

```python
import functools

import jax
import jax.numpy as jnp
import numpy as np
from jax import lax
from jax.experimental import pallas as pl
from jax.experimental.pallas import tpu as pltpu
from jax.sharding import PartitionSpec as P

EX = 2
EY = 2
EZ = 16
ITERS = 4

time_step = 0.25
MESH = pl.DeviceIdType.MESH
f32 = jnp.float32
bf16 = jnp.bfloat16

SIDES = ((-1, 0), (1, 0), (0, -1), (0, 1))


def legendre_seven(points):
    previous = points * 0.0 + 1.0
    current = points
    for degree in range(1, 7):
        following = ((2 * degree + 1) * points * current - degree * previous) / (degree + 1)
        previous = current
        current = following
    return current


def gll_tables():
    poly_order = 7
    points = np.array(
        [
            -1.0,
            -0.8717401485096066,
            -0.5917001814331423,
            -0.2092992179024789,
            0.2092992179024789,
            0.5917001814331423,
            0.8717401485096066,
            1.0,
        ]
    )
    end_values = legendre_seven(points)
    weights = 2.0 / (poly_order * (poly_order + 1) * end_values**2)
    spread = points[:, None] - points[None, :]
    identity = np.eye(poly_order + 1)
    diff_table = end_values[:, None] / (end_values[None, :] * (spread + identity))
    diff_table = diff_table * (1.0 - identity)
    corners = np.zeros(poly_order + 1)
    corners[0] = -poly_order * (poly_order + 1) / 4.0
    corners[-1] = poly_order * (poly_order + 1) / 4.0
    diff_table = diff_table + identity * corners[None, :]
    return (weights.astype(np.float32), diff_table.astype(np.float32))


def constant_tables():
    weights, diff = gll_tables()
    eye = np.eye(8, dtype=np.float32)
    pair = np.eye(2, dtype=np.float32)
    along_j = np.kron(pair, np.kron(diff.T, eye))
    along_k = np.kron(pair, np.kron(eye, diff.T))
    coef = np.zeros((2, 2, 4, 4, 128), np.float32)
    for flip in range(2):
        matrix = diff.T if flip else diff
        for out in range(4):
            for inn in range(4):
                for il in range(2):
                    span = slice(il * 64, il * 64 + 64)
                    coef[flip, 0, out, inn, span] = matrix[2 * out + il, 2 * inn + il]
                    coef[flip, 1, out, inn, span] = matrix[2 * out + il, 2 * inn + 1 - il]
    coef = coef.reshape(64, 128)
    cube = weights[:, None, None] * weights[None, :, None] * weights[None, None, :]
    cube = np.concatenate([cube.reshape(4, 128), np.zeros((4, 128))])
    stack = [along_j, along_k, along_j.T, along_k.T, coef, cube]
    return np.concatenate(stack).astype(np.float32)


def dot(a, b):
    return jnp.dot(a, b, preferred_element_type=f32)


def split(values):
    high = values.astype(bf16)
    return high, (values - high.astype(f32)).astype(bf16)


def roll(values, shift, axis=None):
    axis = values.ndim - 1 if axis is None else axis
    shift = shift % values.shape[axis]
    return values if shift == 0 else pltpu.roll(values, shift, axis)


def kernel(
    nx,
    ny,
    adj_hbm,
    vel_hbm,
    dif_hbm,
    jac_hbm,
    slot_hbm,
    table_hbm,
    out_ref,
    adj_ref,
    vel_ref,
    dif_ref,
    jac_ref,
    slot_ref,
    table,
    forth,
    back,
    mass,
    cond,
    source,
    field,
    base2,
    base3,
    dots,
    face_out,
    face_in,
    early_x,
    early_y,
    late,
    fetch_s,
    face_s,
    face_r,
    sums_s,
    sums_r,
):
    gx = lax.axis_index("gx")
    gy = lax.axis_index("gy")
    total = nx * ny
    me = gx * ny + gy
    cells = EX * EY * EZ

    fetches = [
        pltpu.make_async_copy(there, here, fetch_s.at[at])
        for at, (there, here) in enumerate(
            (
                (slot_hbm, slot_ref),
                (adj_hbm, adj_ref),
                (table_hbm, table),
                (jac_hbm, jac_ref),
                (vel_hbm, vel_ref),
                (dif_hbm, dif_ref),
            )
        )
    ]
    for fetch in fetches:
        fetch.start()
    got_slot, got_adj, got_table, got_jac, got_vel, got_dif = fetches

    face_in[...] = jnp.zeros_like(face_in)

    barrier = pltpu.get_barrier_semaphore()

    def greet(step, carry):
        other = lax.rem(me + step, total)
        pl.semaphore_signal(
            barrier, inc=1, device_id=(other // ny, lax.rem(other, ny)), device_id_type=MESH
        )
        return carry

    lax.fori_loop(1, total, greet, 0)
    dots[...] = jnp.zeros_like(dots)

    lane = lax.broadcasted_iota(jnp.int32, (1, 128), 1)
    lane_j = (lane // 8) % 8
    lane_i = lane // 64

    got_slot.wait()
    place = lax.broadcasted_iota(jnp.int32, (cells, cells), 0)
    picks = (jnp.broadcast_to(slot_ref[...], (cells, cells)) == place).astype(f32)
    pick = picks.astype(bf16)

    pick_both = jnp.concatenate([pick, pick], axis=1)

    def to_brick(stored):
        return dot(pick_both, jnp.concatenate(split(stored), axis=0))

    def derive_jk(values):
        high, low = split(values)
        both = dot(jnp.concatenate([high, low], axis=1), forth[0:256, :])
        both = both + dot(high, forth[256:384, :])
        return both[:, :128], both[:, 128:]

    def derive_i(parts, flip):
        turned = [roll(part, 64) for part in parts]
        outs = []
        for out in range(4):
            acc = None
            for inn in range(4):
                at = 512 + flip * 32 + out * 4 + inn
                term = parts[inn] * table[at : at + 1, :]
                term = term + turned[inn] * table[at + 16 : at + 17, :]
                acc = term if acc is None else acc + term
            outs.append(acc)
        return outs

    def exists(side):
        ax, ay = gx + side[0], gy + side[1]
        return (ax >= 0) & (ax < nx) & (ay >= 0) & (ay < ny)

    def copies(turn, c, sides):
        made = []
        for d, side in enumerate(SIDES):
            if side in sides:
                copy = pltpu.make_async_remote_copy(
                    src_ref=face_out.at[turn, c, d],
                    dst_ref=face_in.at[turn, c, d],
                    send_sem=face_s.at[turn, c, d],
                    recv_sem=face_r.at[turn, c, d],
                    device_id=(gx + side[0], gy + side[1]),
                    device_id_type=MESH,
                )
                made.append((side, copy))
        return made

    def start(turn, c, sides):
        for side, copy in copies(turn, c, sides):
            pl.when(exists(side))(copy.start)

    def await_faces(turn, c, sides):
        for side, copy in copies(turn, c, sides):
            pl.when(exists((-side[0], -side[1])))(copy.wait_recv)

    def fold_inside(values, turn, c):
        dest = field.at[turn]
        zed = lax.broadcasted_iota(jnp.int32, (EZ, 128), 0)
        kay = lax.broadcasted_iota(jnp.int32, (EZ, 128), 1) % 8
        upper = ((kay == 7) & (zed < EZ - 1)).astype(f32)
        lower = ((kay == 0) & (zed > 0)).astype(f32)
        flat = values.reshape(4 * cells, 128)
        stack = (4 * EX * EY, EZ, 128)
        from_next = roll(roll(flat, 7), -1, 0).reshape(stack)
        from_last = roll(roll(flat, -7), 1, 0).reshape(stack)
        summed = flat.reshape(stack) + from_next * upper[None] + from_last * lower[None]
        summed = summed.reshape(4, EX, EY, EZ, 128)
        columns = [summed[:, :, y] for y in range(EY)]
        folded = list(columns)
        for y in range(EY - 1):
            folded[y] = folded[y] + jnp.where(lane_j == 7, roll(columns[y + 1], 56), 0.0)
            folded[y + 1] = folded[y + 1] + jnp.where(lane_j == 0, roll(columns[y], -56), 0.0)
        for y in range(EY):
            dest[c, :, :, y] = folded[y]
        for x in range(EX - 1):
            left = dest[c, 3, x]
            right = dest[c, 0, x + 1]
            dest[c, 3, x] = left + jnp.where(lane_i == 1, roll(right, 64), 0.0)
            dest[c, 0, x + 1] = right + jnp.where(lane_i == 0, roll(left, 64), 0.0)

    def send_x(turn, c):
        left = field[turn, c, 0, 0]
        face_out[turn, c, 0] = jnp.where(lane_i == 0, left[0], roll(left[1], 64))
        right = field[turn, c, 3, EX - 1]
        face_out[turn, c, 1] = jnp.where(lane_i == 0, roll(right[0], 64), right[1])
        start(turn, c, SIDES[:2])

    def pass_on(turn, c):
        await_faces(turn, c, SIDES[:2])
        left = face_in[turn, c, 1]
        right = face_in[turn, c, 0]
        for h, x, arrived, here in ((0, 0, left, 0), (3, EX - 1, right, 1)):
            turned = roll(arrived, 64)
            pair = (arrived, turned) if here == 0 else (turned, arrived)
            for y in range(EY):
                values = field[turn, c, h, x, y]
                field[turn, c, h, x, y] = values + jnp.where(lane_i == here, pair[y], 0.0)
        for d, y, j in ((2, 0, 0), (3, EY - 1, 7)):
            acc = None
            for h in range(4):
                for x in range(EX):
                    part = jnp.where(lane_j == j, field[turn, c, h, x, y], 0.0)
                    part = roll(part, h * 8 + x * 32 - j * 8)
                    acc = part if acc is None else acc + part
            face_out[turn, c, d] = acc
        start(turn, c, SIDES[2:])

    def take_y(turn, c):
        await_faces(turn, c, SIDES[2:])
        for d, y, j in ((3, 0, 0), (2, EY - 1, 7)):
            arrived = face_in[turn, c, d]
            for h in range(4):
                for x in range(EX):
                    part = roll(arrived, j * 8 - h * 8 - x * 32)
                    values = field[turn, c, h, x, y]
                    field[turn, c, h, x, y] = values + jnp.where(lane_j == j, part, 0.0)

    def pass_previous(turn, c):
        before = 3 * turn + c + 2
        pass_on(before // 3, lax.rem(before, 3))

    def operate(values):
        grad_j, grad_k = derive_jk(values.reshape(4 * cells, 128))
        flux_j = grad_j * cond[1].reshape(4 * cells, 128)
        flux_k = grad_k * cond[2].reshape(4 * cells, 128)
        high, low = split(jnp.concatenate([flux_j, flux_k], axis=1))
        both = dot(high, back[...])
        stiff = both[:, :128] + both[:, 128:] + dot(low, back[:, 0:128])
        stiff = stiff.reshape(4, cells, 128)
        grads = derive_i([values[h] for h in range(4)], 0)
        fluxes = [grads[h] * cond[0, h] for h in range(4)]
        backs = derive_i(fluxes, 1)
        return [mass[h] * values[h] + stiff[h] + backs[h] for h in range(4)]

    def load(turn, c):
        return field[turn, c].reshape(4, cells, 128)

    def add_dot(at, first, second):
        acc = dots[at]
        for h in range(4):
            acc = acc + jnp.sum((first[h] * second[h]).reshape(cells // 8, 8, 128), axis=0)
        dots[at] = acc

    def in_row(first, last):
        sums = jnp.sum(jnp.sum(dots[first:last], axis=1), axis=1, keepdims=True)
        spot = lax.broadcasted_iota(jnp.int32, (last - first, 128), 0)
        here = lax.broadcasted_iota(jnp.int32, (last - first, 128), 1)
        return jnp.sum(jnp.where(spot == here, sums, 0.0), axis=0, keepdims=True)

    def spread_sums(row, buffer, at, spot, count, device):
        buffer[spot] = row

        def send(step, carry):
            pltpu.make_async_remote_copy(
                src_ref=buffer.at[spot],
                dst_ref=buffer.at[spot],
                send_sem=sums_s.at[at],
                recv_sem=sums_r.at[at],
                device_id=device(step),
                device_id_type=MESH,
            ).start()
            return carry

        lax.fori_loop(1, count, send, 0)

    def await_sums(buffer, at, count, sems):
        arrived = buffer.at[pl.ds(0, count - 1)]
        pltpu.make_async_copy(arrived, arrived, sems.at[at]).wait()

    def along_x(step):
        return lax.rem(gx + step, nx), gy

    def along_y(step):
        return gx, lax.rem(gy + step, ny)

    def anywhere(step):
        other = lax.rem(me + step, total)
        return other // ny, lax.rem(other, ny)

    got_adj.wait()
    adj = [to_brick(adj_ref[c]) for c in range(3)]
    got_table.wait()
    f_high, f_low = split(jnp.concatenate([table[0:128], table[128:256]], axis=1))
    forth[0:128, :] = f_high
    forth[128:256, :] = f_high
    forth[256:384, :] = f_low
    b_high, b_low = split(table[256:512])
    back[...] = jnp.concatenate([b_high, b_low], axis=1)
    got_jac.wait()
    jac = to_brick(jac_ref[0])
    for h in range(4):
        mass[h] = jac[:, h * 128 : h * 128 + 128] * table[576 + h : 577 + h, :]
    full = [[adj[c][:, h * 128 : h * 128 + 128] for h in range(4)] for c in range(3)]
    grad_j, grad_k, grad_i = [], [], []
    for c in range(3):
        g_j, g_k = derive_jk(jnp.concatenate(full[c], axis=0))
        grad_j.append(g_j.reshape(4, cells, 128))
        grad_k.append(g_k.reshape(4, cells, 128))
        grad_i.append(derive_i(full[c], 0))
    got_vel.wait()
    flow = [dot(pick, vel_ref[c]) for c in range(3)]
    for h in range(4):
        at = slice(h * 128, h * 128 + 128)
        v = [flow[c][:, at] for c in range(3)]
        r = [
            grad_j[2][h] - grad_k[1][h],
            grad_k[0][h] - grad_i[2][h],
            grad_i[1][h] - grad_j[0][h],
        ]
        for c in range(3):
            c1, c2 = (c + 1) % 3, (c + 2) % 3
            value = full[c][h] + time_step * (v[c1] * r[c2] - v[c2] * r[c1])
            source[c, h] = mass[h] * value

    pl.semaphore_wait(barrier, total - 1)

    def first_send(c, carry):
        fold_inside(source[c], 0, c)
        send_x(0, c)
        return carry

    lax.fori_loop(0, 3, first_send, 0)
    pass_on(0, 0)
    pass_on(0, 1)

    got_dif.wait()
    for m in range(3):
        con = to_brick(dif_ref[m])
        for h in range(4):
            weight = time_step * table[576 + h : 577 + h, :]
            cond[m, h] = con[:, h * 128 : h * 128 + 128] * weight

    pass_on(0, 2)

    def turn_0(c, carry):
        take_y(0, c)
        values = load(0, c)
        add_dot(0, values, source[c])
        applied = operate(values)
        add_dot(1, values, applied)
        pl.when(c > 0)(lambda: pass_on(1, c - 1))
        fold_inside(jnp.stack(applied), 1, c)
        send_x(1, c)
        return carry

    lax.fori_loop(0, 3, turn_0, 0)
    spread_sums(in_row(0, 8), early_x, 0, gx, nx, along_x)

    def turn_1(c, carry):
        @pl.when(c == 1)
        def _():
            await_sums(early_x, 0, nx, sums_r)
            spread_sums(jnp.sum(early_x[...], axis=0), early_y, 1, gy, ny, along_y)

        take_y(1, c)
        values = load(1, c)
        applied = operate(values)
        add_dot(8, load(0, c), applied)
        add_dot(9, values, applied)
        pass_previous(1, c)
        fold_inside(jnp.stack(applied), 2, c)
        send_x(2, c)
        return carry

    lax.fori_loop(0, 3, turn_1, 0)
    await_sums(early_y, 1, ny, sums_r)
    early = jnp.sum(early_y[...], axis=0)
    norm = early[:, 0:1]
    first = early[:, 1:2]
    inv = norm / (1.75 * first)

    def turn_2(c, carry):
        take_y(2, c)
        u0, u1, q = load(0, c), load(1, c), load(2, c)
        v1 = inv * u1 - u0
        values = 2.0 * (inv * (inv * q - u1) - v1) - u0
        base2[c] = values
        applied = operate(values)
        add_dot(10, u0, applied)
        add_dot(11, u1, applied)
        add_dot(12, values, applied)
        pass_previous(2, c)
        fold_inside(jnp.stack(applied), 3, c)
        send_x(3, c)
        return carry

    lax.fori_loop(0, 3, turn_2, 0)

    def turn_3(c, carry):
        take_y(3, c)
        u0, u1, v2, q = load(0, c), load(1, c), base2[c], load(3, c)
        values = 2.0 * (inv * q - v2) - (inv * u1 - u0)
        base3[c] = values
        applied = operate(values)
        add_dot(13, u0, applied)
        add_dot(14, u1, applied)
        add_dot(15, v2, applied)
        add_dot(16, values, applied)
        pl.when(c == 0)(lambda: pass_on(3, 2))
        return carry

    lax.fori_loop(0, 3, turn_3, 0)
    spread_sums(in_row(8, 24), late, 2, me, total, anywhere)

    def drain(at, carry):
        for side, copy in copies(at // 3, lax.rem(at, 3), SIDES):
            pl.when(exists(side))(copy.wait_send)
        return carry

    lax.fori_loop(0, 3 * ITERS, drain, 0)
    await_sums(early_x, 0, nx, sums_s)
    await_sums(early_y, 1, ny, sums_s)

    await_sums(late, 2, total, sums_r)
    row = jnp.sum(late[...], axis=0)
    d = [row[:, at : at + 1] for at in range(9)]
    a = inv * first
    g2 = 2.0 * inv * inv * d[0] - 4.0 * a + norm
    g3 = 2.0 * (inv * d[2] - g2) - (a - norm)
    gram = [
        [first, d[0], d[2], d[5]],
        [d[0], d[1], d[3], d[6]],
        [d[2], d[3], d[4], d[7]],
        [d[5], d[6], d[7], d[8]],
    ]
    side = [norm, first, g2, g3]
    diagonal = [gram[at][at] for at in range(4)]
    inverse = []
    for at in range(4):
        pivot = gram[at][at]
        usable = pivot > 1e-6 * diagonal[at]
        inverse.append(jnp.where(usable, 1.0 / pivot, 0.0))
        for below in range(at + 1, 4):
            factor = gram[below][at] * inverse[at]
            for across in range(at + 1, 4):
                gram[below][across] = gram[below][across] - factor * gram[at][across]
            side[below] = side[below] - factor * side[at]
    weights = [None] * 4
    for at in (3, 2, 1, 0):
        value = side[at]
        for across in range(at + 1, 4):
            value = value - gram[at][across] * weights[across]
        weights[at] = value * inverse[at]

    put_back = picks.T.astype(bf16)
    put_back = jnp.concatenate([put_back, put_back], axis=1)
    for c in range(3):
        mixed = weights[0] * load(0, c) + weights[1] * load(1, c)
        mixed = mixed + weights[2] * base2[c] + weights[3] * base3[c]
        whole = jnp.concatenate([mixed[h] for h in range(4)], axis=1)
        out_ref[c] = dot(put_back, jnp.concatenate(split(whole), axis=0))
    await_sums(late, 2, total, sums_s)


def local(nx, ny, adjoint_field, velocity, diffusivity, jacobian, element_slot):
    table = jnp.asarray(constant_tables())
    cells = element_slot.size
    nodes = adjoint_field.shape[-1]
    brick = (3, 4, EX, EY, EZ, 128)
    flat = (3, 4, cells, 128)
    hbm = pl.BlockSpec(memory_space=pltpu.HBM)
    result = pl.pallas_call(
        functools.partial(kernel, nx, ny),
        out_shape=jax.ShapeDtypeStruct((3, cells, nodes), f32),
        in_specs=[hbm] * 6,
        out_specs=pl.BlockSpec(memory_space=pltpu.VMEM),
        scratch_shapes=[
            pltpu.VMEM((3, cells, nodes), f32),
            pltpu.VMEM((3, cells, nodes), bf16),
            pltpu.VMEM((3, cells, nodes), f32),
            pltpu.VMEM((1, cells, nodes), f32),
            pltpu.VMEM((1, cells), jnp.int32),
            pltpu.VMEM(table.shape, f32),
            pltpu.VMEM((384, 256), bf16),
            pltpu.VMEM((256, 256), bf16),
            pltpu.VMEM((4, cells, 128), f32),
            pltpu.VMEM(flat, f32),
            pltpu.VMEM(flat, f32),
            pltpu.VMEM((ITERS,) + brick, f32),
            pltpu.VMEM(flat, f32),
            pltpu.VMEM(flat, f32),
            pltpu.VMEM((24, 8, 128), f32),
            pltpu.VMEM((ITERS, 3, 4, EZ, 128), f32),
            pltpu.VMEM((ITERS, 3, 4, EZ, 128), f32),
            pltpu.VMEM((nx, 1, 128), f32),
            pltpu.VMEM((ny, 1, 128), f32),
            pltpu.VMEM((nx * ny, 1, 128), f32),
            pltpu.SemaphoreType.DMA((6,)),
            pltpu.SemaphoreType.DMA((ITERS, 3, 4)),
            pltpu.SemaphoreType.DMA((ITERS, 3, 4)),
            pltpu.SemaphoreType.DMA((3,)),
            pltpu.SemaphoreType.DMA((3,)),
        ],
        compiler_params=pltpu.CompilerParams(
            collective_id=0, has_side_effects=True
        ),
    )(
        adjoint_field.reshape(3, cells, nodes),
        velocity.reshape(3, cells, nodes),
        diffusivity.reshape(3, cells, nodes),
        jacobian.reshape(1, cells, nodes),
        element_slot.reshape(1, cells),
        table,
    )
    return result.reshape(3, 1, 1, cells, nodes)


def solution(mesh):
    in_specs = (
        P(None, "gx", "gy", None, None),
        P(None, "gx", "gy", None, None),
        P(None, "gx", "gy", None, None),
        P("gx", "gy", None, None),
        P("gx", "gy", None),
    )
    out_specs = P(None, "gx", "gy", None, None)
    run = functools.partial(local, mesh.shape["gx"], mesh.shape["gy"])
    return jax.shard_map(run, mesh=mesh, in_specs=in_specs, out_specs=out_specs, check_vma=False)
```

```python
import functools

import jax
import jax.numpy as jnp
import numpy as np
from jax import lax
from jax.experimental import pallas as pl
from jax.experimental.pallas import tpu as pltpu
from jax.sharding import PartitionSpec as P

EX = 2
EY = 2
EZ = 16
ITERS = 4

time_step = 0.25
MESH = pl.DeviceIdType.MESH
f32 = jnp.float32
bf16 = jnp.bfloat16

SIDES = ((-1, 0), (1, 0), (0, -1), (0, 1))
CORNERS = ((-1, -1), (-1, 1), (1, -1), (1, 1))


def legendre_seven(points):
    previous = points * 0.0 + 1.0
    current = points
    for degree in range(1, 7):
        following = ((2 * degree + 1) * points * current - degree * previous) / (degree + 1)
        previous = current
        current = following
    return current


def gll_tables():
    poly_order = 7
    points = np.array(
        [
            -1.0,
            -0.8717401485096066,
            -0.5917001814331423,
            -0.2092992179024789,
            0.2092992179024789,
            0.5917001814331423,
            0.8717401485096066,
            1.0,
        ]
    )
    end_values = legendre_seven(points)
    weights = 2.0 / (poly_order * (poly_order + 1) * end_values**2)
    spread = points[:, None] - points[None, :]
    identity = np.eye(poly_order + 1)
    diff_table = end_values[:, None] / (end_values[None, :] * (spread + identity))
    diff_table = diff_table * (1.0 - identity)
    corners = np.zeros(poly_order + 1)
    corners[0] = -poly_order * (poly_order + 1) / 4.0
    corners[-1] = poly_order * (poly_order + 1) / 4.0
    diff_table = diff_table + identity * corners[None, :]
    return (weights.astype(np.float32), diff_table.astype(np.float32))


def constant_tables():
    weights, diff = gll_tables()
    eye = np.eye(8, dtype=np.float32)
    pair = np.eye(2, dtype=np.float32)
    along_j = np.kron(pair, np.kron(diff.T, eye))
    along_k = np.kron(pair, np.kron(eye, diff.T))
    coef = np.zeros((2, 2, 4, 4, 128), np.float32)
    for flip in range(2):
        matrix = diff.T if flip else diff
        for out in range(4):
            for inn in range(4):
                for il in range(2):
                    span = slice(il * 64, il * 64 + 64)
                    coef[flip, 0, out, inn, span] = matrix[2 * out + il, 2 * inn + il]
                    coef[flip, 1, out, inn, span] = matrix[2 * out + il, 2 * inn + 1 - il]
    coef = coef.reshape(64, 128)
    cube = weights[:, None, None] * weights[None, :, None] * weights[None, None, :]
    cube = np.concatenate([cube.reshape(4, 128), np.zeros((4, 128))])
    stack = [along_j, along_k, along_j.T, along_k.T, coef, cube]
    return np.concatenate(stack).astype(np.float32)


def dot(a, b):
    return jnp.dot(a, b, preferred_element_type=f32)


def split(values):
    high = values.astype(bf16)
    return high, (values - high.astype(f32)).astype(bf16)


def roll(values, shift, axis=None):
    axis = values.ndim - 1 if axis is None else axis
    shift = shift % values.shape[axis]
    return values if shift == 0 else pltpu.roll(values, shift, axis)


def kernel(
    nx,
    ny,
    adj_hbm,
    vel_hbm,
    dif_hbm,
    jac_hbm,
    slot_hbm,
    table_hbm,
    out_ref,
    adj_ref,
    vel_ref,
    dif_ref,
    jac_ref,
    slot_ref,
    table,
    forth,
    back,
    mass,
    cond,
    source,
    base0,
    base1,
    base2,
    base3,
    passed,
    dots,
    face_out,
    face_in,
    corner_out,
    corner_in,
    early_x,
    early_y,
    late,
    fetch_s,
    face_s,
    face_r,
    corner_s,
    corner_r,
    sums_s,
    sums_r,
):
    gx = lax.axis_index("gx")
    gy = lax.axis_index("gy")
    total = nx * ny
    me = gx * ny + gy
    cells = EX * EY * EZ

    fetches = [
        pltpu.make_async_copy(there, here, fetch_s.at[at])
        for at, (there, here) in enumerate(
            (
                (slot_hbm, slot_ref),
                (adj_hbm, adj_ref),
                (table_hbm, table),
                (jac_hbm, jac_ref),
                (vel_hbm, vel_ref),
                (dif_hbm, dif_ref),
            )
        )
    ]
    for fetch in fetches:
        fetch.start()
    got_slot, got_adj, got_table, got_jac, got_vel, got_dif = fetches

    face_in[...] = jnp.zeros_like(face_in)
    corner_in[...] = jnp.zeros_like(corner_in)

    barrier = pltpu.get_barrier_semaphore()

    def greet(step, carry):
        other = lax.rem(me + step, total)
        pl.semaphore_signal(
            barrier, inc=1, device_id=(other // ny, lax.rem(other, ny)), device_id_type=MESH
        )
        return carry

    lax.fori_loop(1, total, greet, 0)
    dots[...] = jnp.zeros_like(dots)

    lane = lax.broadcasted_iota(jnp.int32, (1, 128), 1)
    lane_j = (lane // 8) % 8
    lane_i = lane // 64
    group = lane // 8

    got_slot.wait()
    place = lax.broadcasted_iota(jnp.int32, (cells, cells), 0)
    picks = (jnp.broadcast_to(slot_ref[...], (cells, cells)) == place).astype(f32)
    pick = picks.astype(bf16)

    pick_both = jnp.concatenate([pick, pick], axis=1)

    def to_brick(stored):
        return dot(pick_both, jnp.concatenate(split(stored), axis=0))

    def derive_jk(values):
        high, low = split(values)
        both = dot(jnp.concatenate([high, low], axis=1), forth[0:256, :])
        both = both + dot(high, forth[256:384, :])
        return both[:, :128], both[:, 128:]

    def derive_i(parts, flip):
        turned = [roll(part, 64) for part in parts]
        outs = []
        for out in range(4):
            acc = None
            for inn in range(4):
                at = 512 + flip * 32 + out * 4 + inn
                term = parts[inn] * table[at : at + 1, :]
                term = term + turned[inn] * table[at + 16 : at + 17, :]
                acc = term if acc is None else acc + term
            outs.append(acc)
        return outs

    def exists(side):
        ax, ay = gx + side[0], gy + side[1]
        return (ax >= 0) & (ax < nx) & (ay >= 0) & (ay < ny)

    def copies(turn, c):
        made = []
        groups = (
            (SIDES, face_out, face_in, face_s, face_r),
            (CORNERS, corner_out, corner_in, corner_s, corner_r),
        )
        for sides, outgoing, incoming, sent, received in groups:
            for d, side in enumerate(sides):
                copy = pltpu.make_async_remote_copy(
                    src_ref=outgoing.at[turn, c, d],
                    dst_ref=incoming.at[turn, c, d],
                    send_sem=sent.at[turn, c, d],
                    recv_sem=received.at[turn, c, d],
                    device_id=(gx + side[0], gy + side[1]),
                    device_id_type=MESH,
                )
                made.append((side, copy))
        return made

    def corner_spot(side):
        h = 0 if side[0] < 0 else 3
        x = 0 if side[0] < 0 else EX - 1
        y = 0 if side[1] < 0 else EY - 1
        start = (0 if side[0] < 0 else 64) + (0 if side[1] < 0 else 56)
        return h, x, y, start

    def fold_inside(values, dest, c):
        zed = lax.broadcasted_iota(jnp.int32, (EZ, 128), 0)
        kay = lax.broadcasted_iota(jnp.int32, (EZ, 128), 1) % 8
        upper = ((kay == 7) & (zed < EZ - 1)).astype(f32)
        lower = ((kay == 0) & (zed > 0)).astype(f32)
        flat = values.reshape(4 * cells, 128)
        stack = (4 * EX * EY, EZ, 128)
        from_next = roll(roll(flat, 7), -1, 0).reshape(stack)
        from_last = roll(roll(flat, -7), 1, 0).reshape(stack)
        summed = flat.reshape(stack) + from_next * upper[None] + from_last * lower[None]
        summed = summed.reshape(4, EX, EY, EZ, 128)
        columns = [summed[:, :, y] for y in range(EY)]
        folded = list(columns)
        for y in range(EY - 1):
            folded[y] = folded[y] + jnp.where(lane_j == 7, roll(columns[y + 1], 56), 0.0)
            folded[y + 1] = folded[y + 1] + jnp.where(lane_j == 0, roll(columns[y], -56), 0.0)
        for y in range(EY):
            dest[c, :, :, y] = folded[y]
        for x in range(EX - 1):
            left = dest[c, 3, x]
            right = dest[c, 0, x + 1]
            dest[c, 3, x] = left + jnp.where(lane_i == 1, roll(right, 64), 0.0)
            dest[c, 0, x + 1] = right + jnp.where(lane_i == 0, roll(left, 64), 0.0)

    def send_faces(turn, dest, c):
        left = dest[c, 0, 0]
        face_out[turn, c, 0] = jnp.where(lane_i == 0, left[0], roll(left[1], 64))
        right = dest[c, 3, EX - 1]
        face_out[turn, c, 1] = jnp.where(lane_i == 0, roll(right[0], 64), right[1])
        for d, y, j in ((2, 0, 0), (3, EY - 1, 7)):
            acc = None
            for h in range(4):
                for x in range(EX):
                    part = jnp.where(lane_j == j, dest[c, h, x, y], 0.0)
                    part = roll(part, h * 8 + x * 32 - j * 8)
                    acc = part if acc is None else acc + part
            face_out[turn, c, d] = acc
        for d, side in enumerate(CORNERS):
            h, x, y, start = corner_spot(side)
            line = jnp.where(group == start // 8, dest[c, h, x, y], 0.0)
            line = pltpu.roll(line, -start % 128, 1, stride=8, stride_axis=0)
            corner_out[turn, c, d] = jnp.sum(line, axis=0, keepdims=True)
        for side, copy in reversed(copies(turn, c)):
            pl.when(exists(side))(copy.start)

    def take_faces(turn, dest, c):
        for side, copy in copies(turn, c):
            pl.when(exists((-side[0], -side[1])))(copy.wait_recv)
        left = face_in[turn, c, 1]
        right = face_in[turn, c, 0]
        for h, x, arrived, here in ((0, 0, left, 0), (3, EX - 1, right, 1)):
            turned = roll(arrived, 64)
            pair = (arrived, turned) if here == 0 else (turned, arrived)
            for y in range(EY):
                dest[c, h, x, y] = dest[c, h, x, y] + jnp.where(lane_i == here, pair[y], 0.0)
        for d, y, j in ((3, 0, 0), (2, EY - 1, 7)):
            arrived = face_in[turn, c, d]
            for h in range(4):
                for x in range(EX):
                    part = roll(arrived, j * 8 - h * 8 - x * 32)
                    dest[c, h, x, y] = dest[c, h, x, y] + jnp.where(lane_j == j, part, 0.0)
        row_of = lax.broadcasted_iota(jnp.int32, (EZ, 128), 0)
        own_group = row_of == lax.broadcasted_iota(jnp.int32, (EZ, 128), 1) // 8
        for d, side in enumerate(CORNERS):
            h, x, y, start = corner_spot((-side[0], -side[1]))
            part = jnp.where(own_group, corner_in[turn, c, d], 0.0)
            for shift in (64, 32, 16, 8):
                part = part + roll(part, shift)
            dest[c, h, x, y] = dest[c, h, x, y] + jnp.where(group == start // 8, part, 0.0)

    def operate(values):
        grad_j, grad_k = derive_jk(values.reshape(4 * cells, 128))
        flux_j = grad_j * cond[1].reshape(4 * cells, 128)
        flux_k = grad_k * cond[2].reshape(4 * cells, 128)
        high, low = split(jnp.concatenate([flux_j, flux_k], axis=1))
        both = dot(high, back[...])
        stiff = both[:, :128] + both[:, 128:] + dot(low, back[:, 0:128])
        stiff = stiff.reshape(4, cells, 128)
        grads = derive_i([values[h] for h in range(4)], 0)
        fluxes = [grads[h] * cond[0, h] for h in range(4)]
        backs = derive_i(fluxes, 1)
        return [mass[h] * values[h] + stiff[h] + backs[h] for h in range(4)]

    def load(ref, c):
        return ref[c].reshape(4, cells, 128)

    def add_dot(at, first, second):
        acc = dots[at]
        for h in range(4):
            acc = acc + jnp.sum((first[h] * second[h]).reshape(cells // 8, 8, 128), axis=0)
        dots[at] = acc

    def in_row(first, last):
        sums = jnp.sum(jnp.sum(dots[first:last], axis=1), axis=1, keepdims=True)
        spot = lax.broadcasted_iota(jnp.int32, (last - first, 128), 0)
        here = lax.broadcasted_iota(jnp.int32, (last - first, 128), 1)
        return jnp.sum(jnp.where(spot == here, sums, 0.0), axis=0, keepdims=True)

    def spread_sums(row, buffer, at, spot, count, device):
        buffer[spot] = row

        def send(step, carry):
            pltpu.make_async_remote_copy(
                src_ref=buffer.at[spot],
                dst_ref=buffer.at[spot],
                send_sem=sums_s.at[at],
                recv_sem=sums_r.at[at],
                device_id=device(step),
                device_id_type=MESH,
            ).start()
            return carry

        lax.fori_loop(1, count, send, 0)

    def await_sums(buffer, at, count, sems):
        arrived = buffer.at[pl.ds(0, count - 1)]
        pltpu.make_async_copy(arrived, arrived, sems.at[at]).wait()

    def along_x(step):
        return lax.rem(gx + step, nx), gy

    def along_y(step):
        return gx, lax.rem(gy + step, ny)

    def anywhere(step):
        other = lax.rem(me + step, total)
        return other // ny, lax.rem(other, ny)

    got_adj.wait()
    adj = [to_brick(adj_ref[c]) for c in range(3)]
    got_table.wait()
    f_high, f_low = split(jnp.concatenate([table[0:128], table[128:256]], axis=1))
    forth[0:128, :] = f_high
    forth[128:256, :] = f_high
    forth[256:384, :] = f_low
    b_high, b_low = split(table[256:512])
    back[...] = jnp.concatenate([b_high, b_low], axis=1)
    got_jac.wait()
    jac = to_brick(jac_ref[0])
    for h in range(4):
        mass[h] = jac[:, h * 128 : h * 128 + 128] * table[576 + h : 577 + h, :]
    full = [[adj[c][:, h * 128 : h * 128 + 128] for h in range(4)] for c in range(3)]
    grad_j, grad_k, grad_i = [], [], []
    for c in range(3):
        g_j, g_k = derive_jk(jnp.concatenate(full[c], axis=0))
        grad_j.append(g_j.reshape(4, cells, 128))
        grad_k.append(g_k.reshape(4, cells, 128))
        grad_i.append(derive_i(full[c], 0))
    got_vel.wait()
    flow = [dot(pick, vel_ref[c]) for c in range(3)]
    for h in range(4):
        at = slice(h * 128, h * 128 + 128)
        v = [flow[c][:, at] for c in range(3)]
        r = [
            grad_j[2][h] - grad_k[1][h],
            grad_k[0][h] - grad_i[2][h],
            grad_i[1][h] - grad_j[0][h],
        ]
        for c in range(3):
            c1, c2 = (c + 1) % 3, (c + 2) % 3
            value = full[c][h] + time_step * (v[c1] * r[c2] - v[c2] * r[c1])
            source[c, h] = mass[h] * value

    pl.semaphore_wait(barrier, total - 1)

    def first_send(c, carry):
        fold_inside(source[c], base0, c)
        send_faces(0, base0, c)
        return carry

    lax.fori_loop(0, 3, first_send, 0)

    got_dif.wait()
    for m in range(3):
        con = to_brick(dif_ref[m])
        for h in range(4):
            weight = time_step * table[576 + h : 577 + h, :]
            cond[m, h] = con[:, h * 128 : h * 128 + 128] * weight

    def turn_0(c, carry):
        take_faces(0, base0, c)
        values = load(base0, c)
        add_dot(0, values, source[c])
        applied = operate(values)
        add_dot(1, values, applied)
        fold_inside(jnp.stack(applied), base1, c)
        send_faces(1, base1, c)
        return carry

    lax.fori_loop(0, 3, turn_0, 0)
    spread_sums(in_row(0, 8), early_x, 0, gx, nx, along_x)

    def turn_1(c, carry):
        @pl.when(c == 1)
        def _():
            await_sums(early_x, 0, nx, sums_r)
            spread_sums(jnp.sum(early_x[...], axis=0), early_y, 1, gy, ny, along_y)

        take_faces(1, base1, c)
        values = load(base1, c)
        applied = operate(values)
        add_dot(8, load(base0, c), applied)
        add_dot(9, values, applied)
        fold_inside(jnp.stack(applied), passed, c)
        send_faces(2, passed, c)
        return carry

    lax.fori_loop(0, 3, turn_1, 0)
    await_sums(early_y, 1, ny, sums_r)
    early = jnp.sum(early_y[...], axis=0)
    norm = early[:, 0:1]
    first = early[:, 1:2]
    inv = norm / (1.75 * first)

    def turn_2(c, carry):
        take_faces(2, passed, c)
        u0, u1, q = load(base0, c), load(base1, c), load(passed, c)
        v1 = inv * u1 - u0
        values = 2.0 * (inv * (inv * q - u1) - v1) - u0
        base2[c] = values
        applied = operate(values)
        add_dot(10, u0, applied)
        add_dot(11, u1, applied)
        add_dot(12, values, applied)
        fold_inside(jnp.stack(applied), passed, c)
        send_faces(3, passed, c)
        return carry

    lax.fori_loop(0, 3, turn_2, 0)

    def turn_3(c, carry):
        take_faces(3, passed, c)
        u0, u1, v2, q = load(base0, c), load(base1, c), base2[c], load(passed, c)
        values = 2.0 * (inv * q - v2) - (inv * u1 - u0)
        base3[c] = values
        applied = operate(values)
        add_dot(13, u0, applied)
        add_dot(14, u1, applied)
        add_dot(15, v2, applied)
        add_dot(16, values, applied)
        return carry

    lax.fori_loop(0, 3, turn_3, 0)
    spread_sums(in_row(8, 24), late, 2, me, total, anywhere)

    def drain(at, carry):
        for side, copy in copies(at // 3, at % 3):
            pl.when(exists(side))(copy.wait_send)
        return carry

    lax.fori_loop(0, 3 * ITERS, drain, 0)
    await_sums(early_x, 0, nx, sums_s)
    await_sums(early_y, 1, ny, sums_s)

    await_sums(late, 2, total, sums_r)
    row = jnp.sum(late[...], axis=0)
    d = [row[:, at : at + 1] for at in range(9)]
    a = inv * first
    g2 = 2.0 * inv * inv * d[0] - 4.0 * a + norm
    g3 = 2.0 * (inv * d[2] - g2) - (a - norm)
    gram = [
        [first, d[0], d[2], d[5]],
        [d[0], d[1], d[3], d[6]],
        [d[2], d[3], d[4], d[7]],
        [d[5], d[6], d[7], d[8]],
    ]
    side = [norm, first, g2, g3]
    diagonal = [gram[at][at] for at in range(4)]
    inverse = []
    for at in range(4):
        pivot = gram[at][at]
        usable = pivot > 1e-6 * diagonal[at]
        inverse.append(jnp.where(usable, 1.0 / pivot, 0.0))
        for below in range(at + 1, 4):
            factor = gram[below][at] * inverse[at]
            for across in range(at + 1, 4):
                gram[below][across] = gram[below][across] - factor * gram[at][across]
            side[below] = side[below] - factor * side[at]
    weights = [None] * 4
    for at in (3, 2, 1, 0):
        value = side[at]
        for across in range(at + 1, 4):
            value = value - gram[at][across] * weights[across]
        weights[at] = value * inverse[at]

    put_back = picks.T.astype(bf16)
    put_back = jnp.concatenate([put_back, put_back], axis=1)
    for c in range(3):
        mixed = weights[0] * load(base0, c) + weights[1] * load(base1, c)
        mixed = mixed + weights[2] * base2[c] + weights[3] * base3[c]
        whole = jnp.concatenate([mixed[h] for h in range(4)], axis=1)
        out_ref[c] = dot(put_back, jnp.concatenate(split(whole), axis=0))
    await_sums(late, 2, total, sums_s)


def local(nx, ny, adjoint_field, velocity, diffusivity, jacobian, element_slot):
    table = jnp.asarray(constant_tables())
    cells = element_slot.size
    nodes = adjoint_field.shape[-1]
    brick = (3, 4, EX, EY, EZ, 128)
    flat = (3, 4, cells, 128)
    hbm = pl.BlockSpec(memory_space=pltpu.HBM)
    result = pl.pallas_call(
        functools.partial(kernel, nx, ny),
        out_shape=jax.ShapeDtypeStruct((3, cells, nodes), f32),
        in_specs=[hbm] * 6,
        out_specs=pl.BlockSpec(memory_space=pltpu.VMEM),
        scratch_shapes=[
            pltpu.VMEM((3, cells, nodes), f32),
            pltpu.VMEM((3, cells, nodes), bf16),
            pltpu.VMEM((3, cells, nodes), f32),
            pltpu.VMEM((1, cells, nodes), f32),
            pltpu.VMEM((1, cells), jnp.int32),
            pltpu.VMEM(table.shape, f32),
            pltpu.VMEM((384, 256), bf16),
            pltpu.VMEM((256, 256), bf16),
            pltpu.VMEM((4, cells, 128), f32),
            pltpu.VMEM(flat, f32),
            pltpu.VMEM(flat, f32),
            pltpu.VMEM(brick, f32),
            pltpu.VMEM(brick, f32),
            pltpu.VMEM(flat, f32),
            pltpu.VMEM(flat, f32),
            pltpu.VMEM(brick, f32),
            pltpu.VMEM((24, 8, 128), f32),
            pltpu.VMEM((ITERS, 3, 4, EZ, 128), f32),
            pltpu.VMEM((ITERS, 3, 4, EZ, 128), f32),
            pltpu.VMEM((ITERS, 3, 4, 1, 128), f32),
            pltpu.VMEM((ITERS, 3, 4, 1, 128), f32),
            pltpu.VMEM((nx, 1, 128), f32),
            pltpu.VMEM((ny, 1, 128), f32),
            pltpu.VMEM((nx * ny, 1, 128), f32),
            pltpu.SemaphoreType.DMA((6,)),
            pltpu.SemaphoreType.DMA((ITERS, 3, 4)),
            pltpu.SemaphoreType.DMA((ITERS, 3, 4)),
            pltpu.SemaphoreType.DMA((ITERS, 3, 4)),
            pltpu.SemaphoreType.DMA((ITERS, 3, 4)),
            pltpu.SemaphoreType.DMA((3,)),
            pltpu.SemaphoreType.DMA((3,)),
        ],
        compiler_params=pltpu.CompilerParams(
            collective_id=0, has_side_effects=True
        ),
    )(
        adjoint_field.reshape(3, cells, nodes),
        velocity.reshape(3, cells, nodes),
        diffusivity.reshape(3, cells, nodes),
        jacobian.reshape(1, cells, nodes),
        element_slot.reshape(1, cells),
        table,
    )
    return result.reshape(3, 1, 1, cells, nodes)


def solution(mesh):
    in_specs = (
        P(None, "gx", "gy", None, None),
        P(None, "gx", "gy", None, None),
        P(None, "gx", "gy", None, None),
        P("gx", "gy", None, None),
        P("gx", "gy", None),
    )
    out_specs = P(None, "gx", "gy", None, None)
    run = functools.partial(local, mesh.shape["gx"], mesh.shape["gy"])
    return jax.shard_map(run, mesh=mesh, in_specs=in_specs, out_specs=out_specs, check_vma=False)
```

```python
import functools

import jax
import jax.numpy as jnp
import numpy as np
from jax import lax
from jax.experimental import pallas as pl
from jax.experimental.pallas import tpu as pltpu
from jax.sharding import PartitionSpec as P

EX = 2
EY = 2
EZ = 16
ITERS = 4

time_step = 0.25
MESH = pl.DeviceIdType.MESH
f32 = jnp.float32
bf16 = jnp.bfloat16

SIDES = ((-1, 0), (1, 0), (0, -1), (0, 1))
CORNERS = ((-1, -1), (-1, 1), (1, -1), (1, 1))


def legendre_seven(points):
    previous = points * 0.0 + 1.0
    current = points
    for degree in range(1, 7):
        following = ((2 * degree + 1) * points * current - degree * previous) / (degree + 1)
        previous = current
        current = following
    return current


def gll_tables():
    poly_order = 7
    points = np.array(
        [
            -1.0,
            -0.8717401485096066,
            -0.5917001814331423,
            -0.2092992179024789,
            0.2092992179024789,
            0.5917001814331423,
            0.8717401485096066,
            1.0,
        ]
    )
    end_values = legendre_seven(points)
    weights = 2.0 / (poly_order * (poly_order + 1) * end_values**2)
    spread = points[:, None] - points[None, :]
    identity = np.eye(poly_order + 1)
    diff_table = end_values[:, None] / (end_values[None, :] * (spread + identity))
    diff_table = diff_table * (1.0 - identity)
    corners = np.zeros(poly_order + 1)
    corners[0] = -poly_order * (poly_order + 1) / 4.0
    corners[-1] = poly_order * (poly_order + 1) / 4.0
    diff_table = diff_table + identity * corners[None, :]
    return (weights.astype(np.float32), diff_table.astype(np.float32))


def constant_tables():
    weights, diff = gll_tables()
    eye = np.eye(8, dtype=np.float32)
    pair = np.eye(2, dtype=np.float32)
    along_j = np.kron(pair, np.kron(diff.T, eye))
    along_k = np.kron(pair, np.kron(eye, diff.T))
    coef = np.zeros((2, 2, 4, 4, 128), np.float32)
    for flip in range(2):
        matrix = diff.T if flip else diff
        for out in range(4):
            for inn in range(4):
                for il in range(2):
                    span = slice(il * 64, il * 64 + 64)
                    coef[flip, 0, out, inn, span] = matrix[2 * out + il, 2 * inn + il]
                    coef[flip, 1, out, inn, span] = matrix[2 * out + il, 2 * inn + 1 - il]
    coef = coef.reshape(64, 128)
    cube = weights[:, None, None] * weights[None, :, None] * weights[None, None, :]
    cube = np.concatenate([cube.reshape(4, 128), np.zeros((4, 128))])
    stack = [along_j, along_k, along_j.T, along_k.T, coef, cube]
    return np.concatenate(stack).astype(np.float32)


def dot(a, b):
    return jnp.dot(a, b, preferred_element_type=f32)


def split(values):
    high = values.astype(bf16)
    return high, (values - high.astype(f32)).astype(bf16)


def roll(values, shift, axis=None):
    axis = values.ndim - 1 if axis is None else axis
    shift = shift % values.shape[axis]
    return values if shift == 0 else pltpu.roll(values, shift, axis)


def kernel(
    nx,
    ny,
    adj_hbm,
    vel_hbm,
    dif_hbm,
    jac_hbm,
    slot_hbm,
    table_hbm,
    out_ref,
    adj_ref,
    vel_ref,
    dif_ref,
    jac_ref,
    slot_ref,
    table,
    forth,
    back,
    mass,
    cond,
    source,
    base0,
    base1,
    base2,
    base3,
    passed,
    dots,
    face_out,
    face_in,
    corner_out,
    corner_in,
    early_x,
    early_y,
    late,
    fetch_s,
    face_s,
    face_r,
    corner_s,
    corner_r,
    sums_s,
    sums_r,
):
    gx = lax.axis_index("gx")
    gy = lax.axis_index("gy")
    total = nx * ny
    me = gx * ny + gy
    cells = EX * EY * EZ

    fetches = [
        pltpu.make_async_copy(there, here, fetch_s.at[at])
        for at, (there, here) in enumerate(
            (
                (slot_hbm, slot_ref),
                (adj_hbm, adj_ref),
                (table_hbm, table),
                (jac_hbm, jac_ref),
                (vel_hbm, vel_ref),
                (dif_hbm, dif_ref),
            )
        )
    ]
    for fetch in fetches:
        fetch.start()
    got_slot, got_adj, got_table, got_jac, got_vel, got_dif = fetches

    face_in[...] = jnp.zeros_like(face_in)
    corner_in[...] = jnp.zeros_like(corner_in)

    barrier = pltpu.get_barrier_semaphore()

    def wrap(at, count):
        return jnp.where(at >= count, at - count, at)

    def everyone_else(act):
        for step in range(1, ny):
            act(gx, wrap(gy + step, ny))

        def column(step, carry):
            other = wrap(gx + step, nx)
            for across in range(ny):
                act(other, wrap(gy + across, ny))
            return carry

        lax.fori_loop(1, nx, column, 0)

    def greet(x, y):
        pl.semaphore_signal(barrier, inc=1, device_id=(x, y), device_id_type=MESH)

    everyone_else(greet)
    dots[...] = jnp.zeros_like(dots)

    lane = lax.broadcasted_iota(jnp.int32, (1, 128), 1)
    lane_j = (lane // 8) % 8
    lane_i = lane // 64
    group = lane // 8

    got_slot.wait()
    place = lax.broadcasted_iota(jnp.int32, (cells, cells), 0)
    picks = (jnp.broadcast_to(slot_ref[...], (cells, cells)) == place).astype(f32)
    pick = picks.astype(bf16)

    pick_both = jnp.concatenate([pick, pick], axis=1)

    def to_brick(stored):
        return dot(pick_both, jnp.concatenate(split(stored), axis=0))

    def derive_jk(values):
        high, low = split(values)
        both = dot(jnp.concatenate([high, low], axis=1), forth[0:256, :])
        both = both + dot(high, forth[256:384, :])
        return both[:, :128], both[:, 128:]

    def derive_i(parts, flip):
        turned = [roll(part, 64) for part in parts]
        outs = []
        for out in range(4):
            acc = None
            for inn in range(4):
                at = 512 + flip * 32 + out * 4 + inn
                term = parts[inn] * table[at : at + 1, :]
                term = term + turned[inn] * table[at + 16 : at + 17, :]
                acc = term if acc is None else acc + term
            outs.append(acc)
        return outs

    def exists(side):
        ax, ay = gx + side[0], gy + side[1]
        return (ax >= 0) & (ax < nx) & (ay >= 0) & (ay < ny)

    def copies(turn, c):
        made = []
        groups = (
            (SIDES, face_out, face_in, face_s, face_r),
            (CORNERS, corner_out, corner_in, corner_s, corner_r),
        )
        for sides, outgoing, incoming, sent, received in groups:
            for d, side in enumerate(sides):
                copy = pltpu.make_async_remote_copy(
                    src_ref=outgoing.at[turn, c, d],
                    dst_ref=incoming.at[turn, c, d],
                    send_sem=sent.at[turn, c, d],
                    recv_sem=received.at[turn, c, d],
                    device_id=(gx + side[0], gy + side[1]),
                    device_id_type=MESH,
                )
                made.append((side, copy))
        return made

    def corner_spot(side):
        h = 0 if side[0] < 0 else 3
        x = 0 if side[0] < 0 else EX - 1
        y = 0 if side[1] < 0 else EY - 1
        start = (0 if side[0] < 0 else 64) + (0 if side[1] < 0 else 56)
        return h, x, y, start

    def fold_inside(values, dest, c):
        zed = lax.broadcasted_iota(jnp.int32, (EZ, 128), 0)
        kay = lax.broadcasted_iota(jnp.int32, (EZ, 128), 1) % 8
        upper = ((kay == 7) & (zed < EZ - 1)).astype(f32)
        lower = ((kay == 0) & (zed > 0)).astype(f32)
        flat = values.reshape(4 * cells, 128)
        stack = (4 * EX * EY, EZ, 128)
        from_next = roll(roll(flat, 7), -1, 0).reshape(stack)
        from_last = roll(roll(flat, -7), 1, 0).reshape(stack)
        summed = flat.reshape(stack) + from_next * upper[None] + from_last * lower[None]
        summed = summed.reshape(4, EX, EY, EZ, 128)
        columns = [summed[:, :, y] for y in range(EY)]
        folded = list(columns)
        for y in range(EY - 1):
            folded[y] = folded[y] + jnp.where(lane_j == 7, roll(columns[y + 1], 56), 0.0)
            folded[y + 1] = folded[y + 1] + jnp.where(lane_j == 0, roll(columns[y], -56), 0.0)
        for y in range(EY):
            dest[c, :, :, y] = folded[y]
        for x in range(EX - 1):
            left = dest[c, 3, x]
            right = dest[c, 0, x + 1]
            dest[c, 3, x] = left + jnp.where(lane_i == 1, roll(right, 64), 0.0)
            dest[c, 0, x + 1] = right + jnp.where(lane_i == 0, roll(left, 64), 0.0)

    def send_faces(turn, dest, c):
        left = dest[c, 0, 0]
        face_out[turn, c, 0] = jnp.where(lane_i == 0, left[0], roll(left[1], 64))
        right = dest[c, 3, EX - 1]
        face_out[turn, c, 1] = jnp.where(lane_i == 0, roll(right[0], 64), right[1])
        for d, y, j in ((2, 0, 0), (3, EY - 1, 7)):
            acc = None
            for h in range(4):
                for x in range(EX):
                    part = jnp.where(lane_j == j, dest[c, h, x, y], 0.0)
                    part = roll(part, h * 8 + x * 32 - j * 8)
                    acc = part if acc is None else acc + part
            face_out[turn, c, d] = acc
        for d, side in enumerate(CORNERS):
            h, x, y, start = corner_spot(side)
            corner_out[turn, c, d] = dest[c, h, x, y]
        for side, copy in copies(turn, c):
            pl.when(exists(side))(copy.start)

    def take_faces(turn, dest, c):
        for side, copy in copies(turn, c):
            pl.when(exists((-side[0], -side[1])))(copy.wait_recv)
        left = face_in[turn, c, 1]
        right = face_in[turn, c, 0]
        for h, x, arrived, here in ((0, 0, left, 0), (3, EX - 1, right, 1)):
            turned = roll(arrived, 64)
            pair = (arrived, turned) if here == 0 else (turned, arrived)
            for y in range(EY):
                dest[c, h, x, y] = dest[c, h, x, y] + jnp.where(lane_i == here, pair[y], 0.0)
        for d, y, j in ((3, 0, 0), (2, EY - 1, 7)):
            arrived = face_in[turn, c, d]
            for h in range(4):
                for x in range(EX):
                    part = roll(arrived, j * 8 - h * 8 - x * 32)
                    dest[c, h, x, y] = dest[c, h, x, y] + jnp.where(lane_j == j, part, 0.0)
        for d, side in enumerate(CORNERS):
            h, x, y, start = corner_spot((-side[0], -side[1]))
            other = corner_spot(side)[3]
            part = roll(corner_in[turn, c, d], start - other)
            dest[c, h, x, y] = dest[c, h, x, y] + jnp.where(group == start // 8, part, 0.0)

    def operate(values):
        grad_j, grad_k = derive_jk(values.reshape(4 * cells, 128))
        flux_j = grad_j * cond[1].reshape(4 * cells, 128)
        flux_k = grad_k * cond[2].reshape(4 * cells, 128)
        high, low = split(jnp.concatenate([flux_j, flux_k], axis=1))
        both = dot(high, back[...])
        stiff = both[:, :128] + both[:, 128:] + dot(low, back[:, 0:128])
        stiff = stiff.reshape(4, cells, 128)
        grads = derive_i([values[h] for h in range(4)], 0)
        fluxes = [grads[h] * cond[0, h] for h in range(4)]
        backs = derive_i(fluxes, 1)
        return [mass[h] * values[h] + stiff[h] + backs[h] for h in range(4)]

    def load(ref, c):
        return ref[c].reshape(4, cells, 128)

    def add_dot(at, first, second):
        acc = dots[at]
        for h in range(4):
            acc = acc + jnp.sum((first[h] * second[h]).reshape(cells // 8, 8, 128), axis=0)
        dots[at] = acc

    def in_row(first, last):
        sums = jnp.sum(jnp.sum(dots[first:last], axis=1), axis=1, keepdims=True)
        spot = lax.broadcasted_iota(jnp.int32, (last - first, 128), 0)
        here = lax.broadcasted_iota(jnp.int32, (last - first, 128), 1)
        return jnp.sum(jnp.where(spot == here, sums, 0.0), axis=0, keepdims=True)

    def spread_sums(row, buffer, at, spot, targets):
        buffer[spot] = row

        def send(x, y):
            pltpu.make_async_remote_copy(
                src_ref=buffer.at[spot],
                dst_ref=buffer.at[spot],
                send_sem=sums_s.at[at],
                recv_sem=sums_r.at[at],
                device_id=(x, y),
                device_id_type=MESH,
            ).start()

        targets(send)

    def await_sums(buffer, at, count, sems):
        arrived = buffer.at[pl.ds(0, count - 1)]
        pltpu.make_async_copy(arrived, arrived, sems.at[at]).wait()

    def along_x(act):
        for step in range(1, nx):
            act(wrap(gx + step, nx), gy)

    def along_y(act):
        for step in range(1, ny):
            act(gx, wrap(gy + step, ny))

    got_adj.wait()
    adj = [to_brick(adj_ref[c]) for c in range(3)]
    got_table.wait()
    f_high, f_low = split(jnp.concatenate([table[0:128], table[128:256]], axis=1))
    forth[0:128, :] = f_high
    forth[128:256, :] = f_high
    forth[256:384, :] = f_low
    b_high, b_low = split(table[256:512])
    back[...] = jnp.concatenate([b_high, b_low], axis=1)
    got_jac.wait()
    jac = to_brick(jac_ref[0])
    for h in range(4):
        mass[h] = jac[:, h * 128 : h * 128 + 128] * table[576 + h : 577 + h, :]
    full = [[adj[c][:, h * 128 : h * 128 + 128] for h in range(4)] for c in range(3)]
    grad_j, grad_k, grad_i = [], [], []
    for c in range(3):
        g_j, g_k = derive_jk(jnp.concatenate(full[c], axis=0))
        grad_j.append(g_j.reshape(4, cells, 128))
        grad_k.append(g_k.reshape(4, cells, 128))
        grad_i.append(derive_i(full[c], 0))
    got_vel.wait()
    flow = [dot(pick, vel_ref[c]) for c in range(3)]
    for h in range(4):
        at = slice(h * 128, h * 128 + 128)
        v = [flow[c][:, at] for c in range(3)]
        r = [
            grad_j[2][h] - grad_k[1][h],
            grad_k[0][h] - grad_i[2][h],
            grad_i[1][h] - grad_j[0][h],
        ]
        for c in range(3):
            c1, c2 = (c + 1) % 3, (c + 2) % 3
            value = full[c][h] + time_step * (v[c1] * r[c2] - v[c2] * r[c1])
            source[c, h] = mass[h] * value

    pl.semaphore_wait(barrier, total - 1)

    def first_send(c, carry):
        fold_inside(source[c], base0, c)
        send_faces(0, base0, c)
        return carry

    lax.fori_loop(0, 3, first_send, 0)

    got_dif.wait()
    for m in range(3):
        con = to_brick(dif_ref[m])
        for h in range(4):
            weight = time_step * table[576 + h : 577 + h, :]
            cond[m, h] = con[:, h * 128 : h * 128 + 128] * weight

    def turn_0(c, carry):
        take_faces(0, base0, c)
        values = load(base0, c)
        add_dot(0, values, source[c])
        applied = operate(values)
        add_dot(1, values, applied)
        fold_inside(jnp.stack(applied), base1, c)
        send_faces(1, base1, c)
        return carry

    lax.fori_loop(0, 3, turn_0, 0)
    spread_sums(in_row(0, 8), early_x, 0, gx, along_x)

    def turn_1(c, carry):
        @pl.when(c == 1)
        def _():
            await_sums(early_x, 0, nx, sums_r)
            spread_sums(jnp.sum(early_x[...], axis=0), early_y, 1, gy, along_y)

        take_faces(1, base1, c)
        values = load(base1, c)
        applied = operate(values)
        add_dot(8, load(base0, c), applied)
        add_dot(9, values, applied)
        fold_inside(jnp.stack(applied), passed, c)
        send_faces(2, passed, c)
        return carry

    lax.fori_loop(0, 3, turn_1, 0)
    await_sums(early_y, 1, ny, sums_r)
    early = jnp.sum(early_y[...], axis=0)
    norm = early[:, 0:1]
    first = early[:, 1:2]
    inv = norm / (1.75 * first)

    def turn_2(c, carry):
        take_faces(2, passed, c)
        u0, u1, q = load(base0, c), load(base1, c), load(passed, c)
        v1 = inv * u1 - u0
        values = 2.0 * (inv * (inv * q - u1) - v1) - u0
        base2[c] = values
        applied = operate(values)
        add_dot(10, u0, applied)
        add_dot(11, u1, applied)
        add_dot(12, values, applied)
        fold_inside(jnp.stack(applied), passed, c)
        send_faces(3, passed, c)
        return carry

    lax.fori_loop(0, 3, turn_2, 0)

    def turn_3(c, carry):
        take_faces(3, passed, c)
        u0, u1, v2, q = load(base0, c), load(base1, c), base2[c], load(passed, c)
        values = 2.0 * (inv * q - v2) - (inv * u1 - u0)
        base3[c] = values
        applied = operate(values)
        add_dot(13, u0, applied)
        add_dot(14, u1, applied)
        add_dot(15, v2, applied)
        add_dot(16, values, applied)
        return carry

    lax.fori_loop(0, 3, turn_3, 0)
    spread_sums(in_row(8, 24), late, 2, me, everyone_else)

    for turn in range(ITERS):

        def drain(c, carry):
            for side, copy in copies(turn, c):
                pl.when(exists(side))(copy.wait_send)
            return carry

        lax.fori_loop(0, 3, drain, 0)
    await_sums(early_x, 0, nx, sums_s)
    await_sums(early_y, 1, ny, sums_s)

    await_sums(late, 2, total, sums_r)
    row = jnp.sum(late[...], axis=0)
    d = [row[:, at : at + 1] for at in range(9)]
    a = inv * first
    g2 = 2.0 * inv * inv * d[0] - 4.0 * a + norm
    g3 = 2.0 * (inv * d[2] - g2) - (a - norm)
    gram = [
        [first, d[0], d[2], d[5]],
        [d[0], d[1], d[3], d[6]],
        [d[2], d[3], d[4], d[7]],
        [d[5], d[6], d[7], d[8]],
    ]
    side = [norm, first, g2, g3]
    diagonal = [gram[at][at] for at in range(4)]
    inverse = []
    for at in range(4):
        pivot = gram[at][at]
        usable = pivot > 1e-6 * diagonal[at]
        inverse.append(jnp.where(usable, 1.0 / pivot, 0.0))
        for below in range(at + 1, 4):
            factor = gram[below][at] * inverse[at]
            for across in range(at + 1, 4):
                gram[below][across] = gram[below][across] - factor * gram[at][across]
            side[below] = side[below] - factor * side[at]
    weights = [None] * 4
    for at in (3, 2, 1, 0):
        value = side[at]
        for across in range(at + 1, 4):
            value = value - gram[at][across] * weights[across]
        weights[at] = value * inverse[at]

    put_back = picks.T.astype(bf16)
    put_back = jnp.concatenate([put_back, put_back], axis=1)
    for c in range(3):
        mixed = weights[0] * load(base0, c) + weights[1] * load(base1, c)
        mixed = mixed + weights[2] * base2[c] + weights[3] * base3[c]
        whole = jnp.concatenate([mixed[h] for h in range(4)], axis=1)
        out_ref[c] = dot(put_back, jnp.concatenate(split(whole), axis=0))
    await_sums(late, 2, total, sums_s)


def local(nx, ny, adjoint_field, velocity, diffusivity, jacobian, element_slot):
    table = jnp.asarray(constant_tables())
    cells = element_slot.size
    nodes = adjoint_field.shape[-1]
    brick = (3, 4, EX, EY, EZ, 128)
    flat = (3, 4, cells, 128)
    hbm = pl.BlockSpec(memory_space=pltpu.HBM)
    result = pl.pallas_call(
        functools.partial(kernel, nx, ny),
        out_shape=jax.ShapeDtypeStruct((3, cells, nodes), f32),
        in_specs=[hbm] * 6,
        out_specs=pl.BlockSpec(memory_space=pltpu.VMEM),
        scratch_shapes=[
            pltpu.VMEM((3, cells, nodes), f32),
            pltpu.VMEM((3, cells, nodes), bf16),
            pltpu.VMEM((3, cells, nodes), f32),
            pltpu.VMEM((1, cells, nodes), f32),
            pltpu.VMEM((1, cells), jnp.int32),
            pltpu.VMEM(table.shape, f32),
            pltpu.VMEM((384, 256), bf16),
            pltpu.VMEM((256, 256), bf16),
            pltpu.VMEM((4, cells, 128), f32),
            pltpu.VMEM(flat, f32),
            pltpu.VMEM(flat, f32),
            pltpu.VMEM(brick, f32),
            pltpu.VMEM(brick, f32),
            pltpu.VMEM(flat, f32),
            pltpu.VMEM(flat, f32),
            pltpu.VMEM(brick, f32),
            pltpu.VMEM((24, 8, 128), f32),
            pltpu.VMEM((ITERS, 3, 4, EZ, 128), f32),
            pltpu.VMEM((ITERS, 3, 4, EZ, 128), f32),
            pltpu.VMEM((ITERS, 3, 4, EZ, 128), f32),
            pltpu.VMEM((ITERS, 3, 4, EZ, 128), f32),
            pltpu.VMEM((nx, 1, 128), f32),
            pltpu.VMEM((ny, 1, 128), f32),
            pltpu.VMEM((nx * ny, 1, 128), f32),
            pltpu.SemaphoreType.DMA((6,)),
            pltpu.SemaphoreType.DMA((ITERS, 3, 4)),
            pltpu.SemaphoreType.DMA((ITERS, 3, 4)),
            pltpu.SemaphoreType.DMA((ITERS, 3, 4)),
            pltpu.SemaphoreType.DMA((ITERS, 3, 4)),
            pltpu.SemaphoreType.DMA((3,)),
            pltpu.SemaphoreType.DMA((3,)),
        ],
        compiler_params=pltpu.CompilerParams(
            collective_id=0, has_side_effects=True
        ),
    )(
        adjoint_field.reshape(3, cells, nodes),
        velocity.reshape(3, cells, nodes),
        diffusivity.reshape(3, cells, nodes),
        jacobian.reshape(1, cells, nodes),
        element_slot.reshape(1, cells),
        table,
    )
    return result.reshape(3, 1, 1, cells, nodes)


def solution(mesh):
    in_specs = (
        P(None, "gx", "gy", None, None),
        P(None, "gx", "gy", None, None),
        P(None, "gx", "gy", None, None),
        P("gx", "gy", None, None),
        P("gx", "gy", None),
    )
    out_specs = P(None, "gx", "gy", None, None)
    run = functools.partial(local, mesh.shape["gx"], mesh.shape["gy"])
    return jax.shard_map(run, mesh=mesh, in_specs=in_specs, out_specs=out_specs, check_vma=False)
```

```python
import functools

import jax
import jax.numpy as jnp
import numpy as np
from jax import lax
from jax.experimental import pallas as pl
from jax.experimental.pallas import tpu as pltpu
from jax.sharding import PartitionSpec as P

EX = 2
EY = 2
EZ = 16
ITERS = 4

time_step = 0.25
MESH = pl.DeviceIdType.MESH
f32 = jnp.float32
bf16 = jnp.bfloat16

SIDES = ((-1, 0), (1, 0), (0, -1), (0, 1))
CORNERS = ((-1, -1), (-1, 1), (1, -1), (1, 1))


def legendre_seven(points):
    previous = points * 0.0 + 1.0
    current = points
    for degree in range(1, 7):
        following = ((2 * degree + 1) * points * current - degree * previous) / (degree + 1)
        previous = current
        current = following
    return current


def gll_tables():
    poly_order = 7
    points = np.array(
        [
            -1.0,
            -0.8717401485096066,
            -0.5917001814331423,
            -0.2092992179024789,
            0.2092992179024789,
            0.5917001814331423,
            0.8717401485096066,
            1.0,
        ]
    )
    end_values = legendre_seven(points)
    weights = 2.0 / (poly_order * (poly_order + 1) * end_values**2)
    spread = points[:, None] - points[None, :]
    identity = np.eye(poly_order + 1)
    diff_table = end_values[:, None] / (end_values[None, :] * (spread + identity))
    diff_table = diff_table * (1.0 - identity)
    corners = np.zeros(poly_order + 1)
    corners[0] = -poly_order * (poly_order + 1) / 4.0
    corners[-1] = poly_order * (poly_order + 1) / 4.0
    diff_table = diff_table + identity * corners[None, :]
    return (weights.astype(np.float32), diff_table.astype(np.float32))


def constant_tables():
    weights, diff = gll_tables()
    eye = np.eye(8, dtype=np.float32)
    pair = np.eye(2, dtype=np.float32)
    along_j = np.kron(pair, np.kron(diff.T, eye))
    along_k = np.kron(pair, np.kron(eye, diff.T))
    coef = np.zeros((2, 2, 4, 4, 128), np.float32)
    for flip in range(2):
        matrix = diff.T if flip else diff
        for out in range(4):
            for inn in range(4):
                for il in range(2):
                    span = slice(il * 64, il * 64 + 64)
                    coef[flip, 0, out, inn, span] = matrix[2 * out + il, 2 * inn + il]
                    coef[flip, 1, out, inn, span] = matrix[2 * out + il, 2 * inn + 1 - il]
    coef = coef.reshape(64, 128)
    cube = weights[:, None, None] * weights[None, :, None] * weights[None, None, :]
    cube = np.concatenate([cube.reshape(4, 128), np.zeros((4, 128))])
    stack = [along_j, along_k, along_j.T, along_k.T, coef, cube]
    return np.concatenate(stack).astype(np.float32)


def dot(a, b):
    return jnp.dot(a, b, preferred_element_type=f32)


def split(values):
    high = values.astype(bf16)
    return high, (values - high.astype(f32)).astype(bf16)


def roll(values, shift, axis=None):
    axis = values.ndim - 1 if axis is None else axis
    shift = shift % values.shape[axis]
    return values if shift == 0 else pltpu.roll(values, shift, axis)


def kernel(
    nx,
    ny,
    adj_hbm,
    vel_hbm,
    dif_hbm,
    jac_hbm,
    slot_hbm,
    table_hbm,
    out_ref,
    adj_ref,
    vel_ref,
    dif_ref,
    jac_ref,
    slot_ref,
    table,
    forth,
    back,
    mass,
    cond,
    source,
    base0,
    base1,
    base2,
    base3,
    passed,
    dots,
    face_out,
    face_in,
    corner_out,
    corner_in,
    early_x,
    early_y,
    late,
    fetch_s,
    face_s,
    face_r,
    corner_s,
    corner_r,
    sums_s,
    sums_r,
):
    gx = lax.axis_index("gx")
    gy = lax.axis_index("gy")
    total = nx * ny
    me = gx * ny + gy
    cells = EX * EY * EZ

    fetches = [
        pltpu.make_async_copy(there, here, fetch_s.at[at])
        for at, (there, here) in enumerate(
            (
                (slot_hbm, slot_ref),
                (adj_hbm, adj_ref),
                (table_hbm, table),
                (jac_hbm, jac_ref),
                (vel_hbm, vel_ref),
                (dif_hbm, dif_ref),
            )
        )
    ]
    for fetch in fetches:
        fetch.start()
    got_slot, got_adj, got_table, got_jac, got_vel, got_dif = fetches

    face_in[...] = jnp.zeros_like(face_in)
    corner_in[...] = jnp.zeros_like(corner_in)

    barrier = pltpu.get_barrier_semaphore()

    def wrap(at, count):
        return jnp.where(at >= count, at - count, at)

    def everyone_else(act):
        for step in range(1, ny):
            act(gx, wrap(gy + step, ny))

        def column(step, carry):
            other = wrap(gx + step, nx)
            for across in range(ny):
                act(other, wrap(gy + across, ny))
            return carry

        lax.fori_loop(1, nx, column, 0)

    def greet(x, y):
        pl.semaphore_signal(barrier, inc=1, device_id=(x, y), device_id_type=MESH)

    everyone_else(greet)
    dots[...] = jnp.zeros_like(dots)

    lane = lax.broadcasted_iota(jnp.int32, (1, 128), 1)
    lane_j = (lane // 8) % 8
    lane_i = lane // 64
    group = lane // 8

    got_slot.wait()
    place = lax.broadcasted_iota(jnp.int32, (cells, cells), 0)
    picks = (jnp.broadcast_to(slot_ref[...], (cells, cells)) == place).astype(f32)
    pick = picks.astype(bf16)

    pick_both = jnp.concatenate([pick, pick], axis=1)

    def to_brick(stored):
        return dot(pick_both, jnp.concatenate(split(stored), axis=0))

    def derive_jk(values):
        high, low = split(values)
        both = dot(jnp.concatenate([high, low], axis=1), forth[0:256, :])
        both = both + dot(high, forth[256:384, :])
        return both[:, :128], both[:, 128:]

    def derive_i(parts, flip):
        turned = [roll(part, 64) for part in parts]
        outs = []
        for out in range(4):
            acc = None
            for inn in range(4):
                at = 512 + flip * 32 + out * 4 + inn
                term = parts[inn] * table[at : at + 1, :]
                term = term + turned[inn] * table[at + 16 : at + 17, :]
                acc = term if acc is None else acc + term
            outs.append(acc)
        return outs

    def exists(side):
        ax, ay = gx + side[0], gy + side[1]
        return (ax >= 0) & (ax < nx) & (ay >= 0) & (ay < ny)

    def copies(turn, c):
        made = []
        groups = (
            (SIDES, face_out, face_in, face_s, face_r),
            (CORNERS, corner_out, corner_in, corner_s, corner_r),
        )
        for sides, outgoing, incoming, sent, received in groups:
            for d, side in enumerate(sides):
                copy = pltpu.make_async_remote_copy(
                    src_ref=outgoing.at[turn, c, d],
                    dst_ref=incoming.at[turn, c, d],
                    send_sem=sent.at[turn, c, d],
                    recv_sem=received.at[turn, c, d],
                    device_id=(gx + side[0], gy + side[1]),
                    device_id_type=MESH,
                )
                made.append((side, copy))
        return made

    def corner_spot(side):
        h = 0 if side[0] < 0 else 3
        x = 0 if side[0] < 0 else EX - 1
        y = 0 if side[1] < 0 else EY - 1
        start = (0 if side[0] < 0 else 64) + (0 if side[1] < 0 else 56)
        return h, x, y, start

    def fold_inside(values, dest, c):
        zed = lax.broadcasted_iota(jnp.int32, (EZ, 128), 0)
        kay = lax.broadcasted_iota(jnp.int32, (EZ, 128), 1) % 8
        upper = ((kay == 7) & (zed < EZ - 1)).astype(f32)
        lower = ((kay == 0) & (zed > 0)).astype(f32)
        flat = values.reshape(4 * cells, 128)
        stack = (4 * EX * EY, EZ, 128)
        from_next = roll(roll(flat, 7), -1, 0).reshape(stack)
        from_last = roll(roll(flat, -7), 1, 0).reshape(stack)
        summed = flat.reshape(stack) + from_next * upper[None] + from_last * lower[None]
        summed = summed.reshape(4, EX, EY, EZ, 128)
        columns = [summed[:, :, y] for y in range(EY)]
        folded = list(columns)
        for y in range(EY - 1):
            folded[y] = folded[y] + jnp.where(lane_j == 7, roll(columns[y + 1], 56), 0.0)
            folded[y + 1] = folded[y + 1] + jnp.where(lane_j == 0, roll(columns[y], -56), 0.0)
        for y in range(EY):
            dest[c, :, :, y] = folded[y]
        for x in range(EX - 1):
            left = dest[c, 3, x]
            right = dest[c, 0, x + 1]
            dest[c, 3, x] = left + jnp.where(lane_i == 1, roll(right, 64), 0.0)
            dest[c, 0, x + 1] = right + jnp.where(lane_i == 0, roll(left, 64), 0.0)

    def send_faces(turn, dest, c):
        left = dest[c, 0, 0]
        face_out[turn, c, 0] = jnp.where(lane_i == 0, left[0], roll(left[1], 64))
        right = dest[c, 3, EX - 1]
        face_out[turn, c, 1] = jnp.where(lane_i == 0, roll(right[0], 64), right[1])
        for d, y, j in ((2, 0, 0), (3, EY - 1, 7)):
            acc = None
            for h in range(4):
                for x in range(EX):
                    part = jnp.where(lane_j == j, dest[c, h, x, y], 0.0)
                    part = roll(part, h * 8 + x * 32 - j * 8)
                    acc = part if acc is None else acc + part
            face_out[turn, c, d] = acc
        for d, side in enumerate(CORNERS):
            h, x, y, start = corner_spot(side)
            corner_out[turn, c, d] = dest[c, h, x, y]
        for side, copy in copies(turn, c):
            pl.when(exists(side))(copy.start)

    def take_faces(turn, dest, c):
        for side, copy in copies(turn, c):
            pl.when(exists((-side[0], -side[1])))(copy.wait_recv)
        left = face_in[turn, c, 1]
        right = face_in[turn, c, 0]
        for h, x, arrived, here in ((0, 0, left, 0), (3, EX - 1, right, 1)):
            turned = roll(arrived, 64)
            pair = (arrived, turned) if here == 0 else (turned, arrived)
            for y in range(EY):
                dest[c, h, x, y] = dest[c, h, x, y] + jnp.where(lane_i == here, pair[y], 0.0)
        for d, y, j in ((3, 0, 0), (2, EY - 1, 7)):
            arrived = face_in[turn, c, d]
            for h in range(4):
                for x in range(EX):
                    part = roll(arrived, j * 8 - h * 8 - x * 32)
                    dest[c, h, x, y] = dest[c, h, x, y] + jnp.where(lane_j == j, part, 0.0)
        for d, side in enumerate(CORNERS):
            h, x, y, start = corner_spot((-side[0], -side[1]))
            other = corner_spot(side)[3]
            part = roll(corner_in[turn, c, d], start - other)
            dest[c, h, x, y] = dest[c, h, x, y] + jnp.where(group == start // 8, part, 0.0)

    def operate(values):
        grad_j, grad_k = derive_jk(values.reshape(4 * cells, 128))
        flux_j = grad_j * cond[1].reshape(4 * cells, 128)
        flux_k = grad_k * cond[2].reshape(4 * cells, 128)
        high, low = split(jnp.concatenate([flux_j, flux_k], axis=1))
        both = dot(high, back[...])
        stiff = both[:, :128] + both[:, 128:] + dot(low, back[:, 0:128])
        stiff = stiff.reshape(4, cells, 128)
        grads = derive_i([values[h] for h in range(4)], 0)
        fluxes = [grads[h] * cond[0, h] for h in range(4)]
        backs = derive_i(fluxes, 1)
        return [mass[h] * values[h] + stiff[h] + backs[h] for h in range(4)]

    def load(ref, c):
        return ref[c].reshape(4, cells, 128)

    def add_dot(at, first, second):
        acc = dots[at]
        for h in range(4):
            acc = acc + jnp.sum((first[h] * second[h]).reshape(cells // 8, 8, 128), axis=0)
        dots[at] = acc

    def in_row(first, last):
        sums = jnp.sum(jnp.sum(dots[first:last], axis=1), axis=1, keepdims=True)
        spot = lax.broadcasted_iota(jnp.int32, (last - first, 128), 0)
        here = lax.broadcasted_iota(jnp.int32, (last - first, 128), 1)
        return jnp.sum(jnp.where(spot == here, sums, 0.0), axis=0, keepdims=True)

    def spread_sums(row, buffer, at, spot, targets):
        buffer[spot] = row

        def send(x, y):
            pltpu.make_async_remote_copy(
                src_ref=buffer.at[spot],
                dst_ref=buffer.at[spot],
                send_sem=sums_s.at[at],
                recv_sem=sums_r.at[at],
                device_id=(x, y),
                device_id_type=MESH,
            ).start()

        targets(send)

    def await_sums(buffer, at, count, sems):
        arrived = buffer.at[pl.ds(0, count - 1)]
        pltpu.make_async_copy(arrived, arrived, sems.at[at]).wait()

    def along_x(act):
        for step in range(1, nx):
            act(wrap(gx + step, nx), gy)

    def along_y(act):
        for step in range(1, ny):
            act(gx, wrap(gy + step, ny))

    got_adj.wait()
    adj = [to_brick(adj_ref[c]) for c in range(3)]
    got_table.wait()
    f_high, f_low = split(jnp.concatenate([table[0:128], table[128:256]], axis=1))
    forth[0:128, :] = f_high
    forth[128:256, :] = f_high
    forth[256:384, :] = f_low
    b_high, b_low = split(table[256:512])
    back[...] = jnp.concatenate([b_high, b_low], axis=1)
    got_jac.wait()
    jac = to_brick(jac_ref[0])
    for h in range(4):
        mass[h] = jac[:, h * 128 : h * 128 + 128] * table[576 + h : 577 + h, :]
    full = [[adj[c][:, h * 128 : h * 128 + 128] for h in range(4)] for c in range(3)]
    grad_j, grad_k, grad_i = [], [], []
    for c in range(3):
        g_j, g_k = derive_jk(jnp.concatenate(full[c], axis=0))
        grad_j.append(g_j.reshape(4, cells, 128))
        grad_k.append(g_k.reshape(4, cells, 128))
        grad_i.append(derive_i(full[c], 0))
    got_vel.wait()
    flow = [dot(pick, vel_ref[c]) for c in range(3)]
    for h in range(4):
        at = slice(h * 128, h * 128 + 128)
        v = [flow[c][:, at] for c in range(3)]
        r = [
            grad_j[2][h] - grad_k[1][h],
            grad_k[0][h] - grad_i[2][h],
            grad_i[1][h] - grad_j[0][h],
        ]
        for c in range(3):
            c1, c2 = (c + 1) % 3, (c + 2) % 3
            value = full[c][h] + time_step * (v[c1] * r[c2] - v[c2] * r[c1])
            source[c, h] = mass[h] * value

    pl.semaphore_wait(barrier, total - 1)

    def first_send(c, carry):
        fold_inside(source[c], base0, c)
        send_faces(0, base0, c)
        return carry

    for c in range(3):
        first_send(c, 0)

    got_dif.wait()
    for m in range(3):
        con = to_brick(dif_ref[m])
        for h in range(4):
            weight = time_step * table[576 + h : 577 + h, :]
            cond[m, h] = con[:, h * 128 : h * 128 + 128] * weight

    def turn_0(c, carry):
        take_faces(0, base0, c)
        values = load(base0, c)
        add_dot(0, values, source[c])
        applied = operate(values)
        add_dot(1, values, applied)
        fold_inside(jnp.stack(applied), base1, c)
        send_faces(1, base1, c)
        return carry

    for c in range(3):
        turn_0(c, 0)
    spread_sums(in_row(0, 8), early_x, 0, gx, along_x)

    def turn_1(c, carry):
        @pl.when(c == 1)
        def _():
            await_sums(early_x, 0, nx, sums_r)
            spread_sums(jnp.sum(early_x[...], axis=0), early_y, 1, gy, along_y)

        take_faces(1, base1, c)
        values = load(base1, c)
        applied = operate(values)
        add_dot(8, load(base0, c), applied)
        add_dot(9, values, applied)
        fold_inside(jnp.stack(applied), passed, c)
        send_faces(2, passed, c)
        return carry

    for c in range(3):
        turn_1(c, 0)
    await_sums(early_y, 1, ny, sums_r)
    early = jnp.sum(early_y[...], axis=0)
    norm = early[:, 0:1]
    first = early[:, 1:2]
    inv = norm / (1.75 * first)

    def turn_2(c, carry):
        take_faces(2, passed, c)
        u0, u1, q = load(base0, c), load(base1, c), load(passed, c)
        v1 = inv * u1 - u0
        values = 2.0 * (inv * (inv * q - u1) - v1) - u0
        base2[c] = values
        applied = operate(values)
        add_dot(10, u0, applied)
        add_dot(11, u1, applied)
        add_dot(12, values, applied)
        fold_inside(jnp.stack(applied), passed, c)
        send_faces(3, passed, c)
        return carry

    for c in range(3):
        turn_2(c, 0)

    def turn_3(c, carry):
        take_faces(3, passed, c)
        u0, u1, v2, q = load(base0, c), load(base1, c), base2[c], load(passed, c)
        values = 2.0 * (inv * q - v2) - (inv * u1 - u0)
        base3[c] = values
        applied = operate(values)
        add_dot(13, u0, applied)
        add_dot(14, u1, applied)
        add_dot(15, v2, applied)
        add_dot(16, values, applied)
        return carry

    for c in range(3):
        turn_3(c, 0)
    spread_sums(in_row(8, 24), late, 2, me, everyone_else)

    for turn in range(ITERS):

        def drain(c, carry):
            for side, copy in copies(turn, c):
                pl.when(exists(side))(copy.wait_send)
            return carry

        lax.fori_loop(0, 3, drain, 0)
    await_sums(early_x, 0, nx, sums_s)
    await_sums(early_y, 1, ny, sums_s)

    await_sums(late, 2, total, sums_r)
    row = jnp.sum(late[...], axis=0)
    d = [row[:, at : at + 1] for at in range(9)]
    a = inv * first
    g2 = 2.0 * inv * inv * d[0] - 4.0 * a + norm
    g3 = 2.0 * (inv * d[2] - g2) - (a - norm)
    gram = [
        [first, d[0], d[2], d[5]],
        [d[0], d[1], d[3], d[6]],
        [d[2], d[3], d[4], d[7]],
        [d[5], d[6], d[7], d[8]],
    ]
    side = [norm, first, g2, g3]
    diagonal = [gram[at][at] for at in range(4)]
    inverse = []
    for at in range(4):
        pivot = gram[at][at]
        usable = pivot > 1e-6 * diagonal[at]
        inverse.append(jnp.where(usable, 1.0 / pivot, 0.0))
        for below in range(at + 1, 4):
            factor = gram[below][at] * inverse[at]
            for across in range(at + 1, 4):
                gram[below][across] = gram[below][across] - factor * gram[at][across]
            side[below] = side[below] - factor * side[at]
    weights = [None] * 4
    for at in (3, 2, 1, 0):
        value = side[at]
        for across in range(at + 1, 4):
            value = value - gram[at][across] * weights[across]
        weights[at] = value * inverse[at]

    put_back = picks.T.astype(bf16)
    put_back = jnp.concatenate([put_back, put_back], axis=1)
    for c in range(3):
        mixed = weights[0] * load(base0, c) + weights[1] * load(base1, c)
        mixed = mixed + weights[2] * base2[c] + weights[3] * base3[c]
        whole = jnp.concatenate([mixed[h] for h in range(4)], axis=1)
        out_ref[c] = dot(put_back, jnp.concatenate(split(whole), axis=0))
    await_sums(late, 2, total, sums_s)


def local(nx, ny, adjoint_field, velocity, diffusivity, jacobian, element_slot):
    table = jnp.asarray(constant_tables())
    cells = element_slot.size
    nodes = adjoint_field.shape[-1]
    brick = (3, 4, EX, EY, EZ, 128)
    flat = (3, 4, cells, 128)
    hbm = pl.BlockSpec(memory_space=pltpu.HBM)
    result = pl.pallas_call(
        functools.partial(kernel, nx, ny),
        out_shape=jax.ShapeDtypeStruct((3, cells, nodes), f32),
        in_specs=[hbm] * 6,
        out_specs=pl.BlockSpec(memory_space=pltpu.VMEM),
        scratch_shapes=[
            pltpu.VMEM((3, cells, nodes), f32),
            pltpu.VMEM((3, cells, nodes), bf16),
            pltpu.VMEM((3, cells, nodes), f32),
            pltpu.VMEM((1, cells, nodes), f32),
            pltpu.VMEM((1, cells), jnp.int32),
            pltpu.VMEM(table.shape, f32),
            pltpu.VMEM((384, 256), bf16),
            pltpu.VMEM((256, 256), bf16),
            pltpu.VMEM((4, cells, 128), f32),
            pltpu.VMEM(flat, f32),
            pltpu.VMEM(flat, f32),
            pltpu.VMEM(brick, f32),
            pltpu.VMEM(brick, f32),
            pltpu.VMEM(flat, f32),
            pltpu.VMEM(flat, f32),
            pltpu.VMEM(brick, f32),
            pltpu.VMEM((24, 8, 128), f32),
            pltpu.VMEM((ITERS, 3, 4, EZ, 128), f32),
            pltpu.VMEM((ITERS, 3, 4, EZ, 128), f32),
            pltpu.VMEM((ITERS, 3, 4, EZ, 128), f32),
            pltpu.VMEM((ITERS, 3, 4, EZ, 128), f32),
            pltpu.VMEM((nx, 1, 128), f32),
            pltpu.VMEM((ny, 1, 128), f32),
            pltpu.VMEM((nx * ny, 1, 128), f32),
            pltpu.SemaphoreType.DMA((6,)),
            pltpu.SemaphoreType.DMA((ITERS, 3, 4)),
            pltpu.SemaphoreType.DMA((ITERS, 3, 4)),
            pltpu.SemaphoreType.DMA((ITERS, 3, 4)),
            pltpu.SemaphoreType.DMA((ITERS, 3, 4)),
            pltpu.SemaphoreType.DMA((3,)),
            pltpu.SemaphoreType.DMA((3,)),
        ],
        compiler_params=pltpu.CompilerParams(
            collective_id=0, has_side_effects=True
        ),
    )(
        adjoint_field.reshape(3, cells, nodes),
        velocity.reshape(3, cells, nodes),
        diffusivity.reshape(3, cells, nodes),
        jacobian.reshape(1, cells, nodes),
        element_slot.reshape(1, cells),
        table,
    )
    return result.reshape(3, 1, 1, cells, nodes)


def solution(mesh):
    in_specs = (
        P(None, "gx", "gy", None, None),
        P(None, "gx", "gy", None, None),
        P(None, "gx", "gy", None, None),
        P("gx", "gy", None, None),
        P("gx", "gy", None),
    )
    out_specs = P(None, "gx", "gy", None, None)
    run = functools.partial(local, mesh.shape["gx"], mesh.shape["gy"])
    return jax.shard_map(run, mesh=mesh, in_specs=in_specs, out_specs=out_specs, check_vma=False)
```
